128 devices in a mesh: row: 16 (over x, y_lo, core), col: 8 (over y_hi, z).
Axes of the slice: x: 4, y: 4 (y_hi: 2, y_lo: 2; y = y_hi * 2 + y_lo), z: 4, core: 2. Of those that a mesh axis runs over, the one named last changes fastest.
Arguments:
- features: bfloat16 [65536, 256], P(('row', 'col')), may hold values from -6 to 6
- weight: bfloat16 [256, 256], replicated, may hold values from -0.375 to 0.375
- cotangent: bfloat16 [65536, 256], P(('col', 'row')), may hold values from -6 to 6
- block_rows: int32 [16, 8, 384], P('row', 'col'), may hold values from 0 to 63
- block_cols: int32 [16, 8, 384], P('row', 'col'), may hold values from 0 to 31
- counts: int32 [16, 8], P('row', 'col'), may hold values from 64 to 384, as said below
- values: bfloat16 [16, 8, 384, 128, 128], P('row', 'col'), may hold values from -0.078125 to 0.078125
Outputs:
- output: bfloat16 [65536, 256], P(('col', 'row'))
- grad_weight: float32 [256, 256], replicated
- grad_features: bfloat16 [65536, 256], P(('row', 'col'))
The draws below stay inside these ranges and needn't reach their ends.
Inputs may be any that keep to these rules, and one draw needn't show every extreme that they name: `counts`: at least one tile holds 384 blocks.
All inputs are finite; a program needn't handle non-finite values.
Results may differ from the reference program's by a relative error of at most 0.0049.
Values may be sent and summed in bfloat16 or wider, within the bound.
A program may use at most 128 MiB of HBM per device.

```python
import jax
import jax.numpy as jnp
from jax import lax

F = 256
BLOCK = 128
BLK_DEV = 4
NNZ = 384
GROUP = 64
NODES = 65536
N_ROW = 16
N_COL = 8


def draw_counts(key, part):
    key = jax.random.fold_in(key, 7)
    first_key, second_key = jax.random.split(key)
    divisor = 1 + jax.random.randint(first_key, (N_ROW * N_COL,), 0, 6)
    tile_counts = NNZ // divisor
    spot = jax.random.randint(second_key, (), 0, N_ROW * N_COL)
    tile_counts = jnp.where(jnp.arange(N_ROW * N_COL) == spot, NNZ, tile_counts)
    return tile_counts.reshape(N_ROW, N_COL).astype(jnp.int32)


def place_ends(values, key, low, high):
    spot = [jax.random.randint(jax.random.fold_in(key, axis), (), 0, length) for axis, length in enumerate(values.shape)]
    widest = values.shape.index(max(values.shape))
    next_to = spot[:widest] + [(spot[widest] + 1) % values.shape[widest]] + spot[widest + 1:]
    return values.at[tuple(spot)].set(low).at[tuple(next_to)].set(high)


def levels(key, shape, shards, least, largest):
    loudness = 1.0
    for dim, shards_of in shards:
        draws = jax.random.uniform(jax.random.fold_in(jax.random.fold_in(key, 6), dim), (shards_of,), jnp.float32, least / len(shards), largest / len(shards))
        loudness = loudness * jnp.repeat(jnp.exp(draws), shape[dim] // shards_of).reshape((-1,) + (1,) * (len(shape) - 1 - dim))
    return loudness


def centred(stream_key, extent, scale, most, cuts=(), kind=jnp.bfloat16):
    array = jax.random.normal(stream_key, extent, jnp.float32) * scale
    if len(cuts) > 0:
        array = levels(stream_key, extent, cuts, -0.22, 0.18) * array
    return jnp.clip(array, min=-most, max=most).astype(kind)


def setup_inputs(seed: int = 0) -> dict:
    arg_keys = jax.random.split(jax.random.key(seed), 8)
    return {
        "features": centred(arg_keys[0], (NODES, F), 1.0, 6.0, ((0, 128),)),
        "weight": centred(arg_keys[1], (F, F), F ** -0.5, 0.375),
        "cotangent": centred(arg_keys[2], (NODES, F), 1.0, 6.0, ((0, 128),)),
        "block_rows": place_ends(jax.random.randint(arg_keys[3], (N_ROW, N_COL, NNZ), 0, BLK_DEV * N_ROW), jax.random.fold_in(arg_keys[3], 1), 0, (BLK_DEV * N_ROW) - 1).astype(jnp.int32),
        "block_cols": place_ends(jax.random.randint(arg_keys[4], (N_ROW, N_COL, NNZ), 0, BLK_DEV * N_COL), jax.random.fold_in(arg_keys[4], 1), 0, (BLK_DEV * N_COL) - 1).astype(jnp.int32),
        "counts": draw_counts(jax.random.fold_in(arg_keys[7], 71), 0),
        "values": centred(arg_keys[6], (N_ROW, N_COL, NNZ, BLOCK, BLOCK), (NNZ * BLOCK // (2 * BLK_DEV)) ** -0.5, 0.078125, ((0, 16), (1, 8))),
    }


def reference(features, weight, cotangent, block_rows, block_cols, counts, values):
    nodes = features.shape[0]
    width = features.shape[1]
    block = values.shape[-1]
    row_blocks = BLK_DEV * N_ROW
    col_blocks = BLK_DEV * N_COL
    tiles = N_ROW * N_COL
    flat_values = values.reshape(tiles, NNZ, block, block)
    flat_rows = block_rows.reshape(tiles, NNZ).astype(jnp.int32)
    flat_cols = block_cols.reshape(tiles, NNZ).astype(jnp.int32)
    flat_counts = counts.reshape(tiles).astype(jnp.int32)

    def sweep(source, flipped):
        source_blocks = source.astype(jnp.float32).reshape(-1, block, width)

        def per_tile(tile, total):
            tile = jnp.asarray(tile).astype(jnp.int32)
            grid_row = tile // N_COL
            grid_col = tile % N_COL
            tile_values = lax.dynamic_index_in_dim(flat_values, tile, 0, False)
            global_rows = lax.dynamic_index_in_dim(flat_rows, tile, 0, False) + grid_col * row_blocks
            global_cols = lax.dynamic_index_in_dim(flat_cols, tile, 0, False) + grid_row * col_blocks
            count = lax.dynamic_index_in_dim(flat_counts, tile, 0, False)
            target_all = global_cols if flipped else global_rows
            anchor_all = global_rows if flipped else global_cols
            form = "kji,kjf->kif" if flipped else "kij,kjf->kif"

            def advance(index, inner):
                start = (jnp.asarray(index) * GROUP).astype(jnp.int32)
                pieces = lax.dynamic_slice_in_dim(tile_values, start, GROUP, 0).astype(jnp.float32)
                target = lax.dynamic_slice_in_dim(target_all, start, GROUP, 0)
                anchor = lax.dynamic_slice_in_dim(anchor_all, start, GROUP, 0)
                active = (start + jnp.arange(GROUP, dtype=jnp.int32)) < count
                picked = jnp.take(source_blocks, anchor, axis=0)
                product = jnp.einsum(form, pieces, picked, precision=lax.Precision.HIGHEST)
                product = jnp.where(active[:, None, None], product, jnp.float32(0.0))
                return inner.at[target].add(product)

            return lax.fori_loop(0, NNZ // GROUP, advance, total)

        total = jnp.zeros((nodes // block, block, width), jnp.float32)
        total = lax.fori_loop(0, tiles, per_tile, total)
        return total.reshape(nodes, width)

    aggregate = sweep(features, False).astype(jnp.bfloat16)
    output = jnp.dot(aggregate, weight, preferred_element_type=jnp.float32).astype(jnp.bfloat16)
    grad_weight = jnp.dot(aggregate.T, cotangent, preferred_element_type=jnp.float32) * (float(nodes) ** -0.5)
    grad_aggregate = jnp.dot(cotangent, weight.T, preferred_element_type=jnp.float32).astype(jnp.bfloat16)
    grad_features = sweep(grad_aggregate, True).astype(jnp.bfloat16)
    return output, grad_weight, grad_features
```

```python
import functools

import jax
import jax.numpy as jnp
from jax import lax
from jax.experimental import pallas as pl
from jax.experimental.pallas import tpu as pltpu
from jax.sharding import PartitionSpec as P

MESH = pl.DeviceIdType.MESH
BF = jnp.bfloat16
F32 = jnp.float32
B = 128
NNZ = 384
SLOTS = 512
F_PAIRS = 224
B_PAIRS = 208
CHUNK = 4


def meta_kernel(rows_ref, cols_ref, count_ref, blk_f, src_f, keep_f, end_f, has_f, blk_b, src_b, keep_b, end_b, has_b):
    count = count_ref[0, 0]
    lane_k = lax.broadcasted_iota(jnp.int32, (1, NNZ), 1)
    valid = lane_k < count
    rows = jnp.where(valid, rows_ref[...], 900).astype(F32)
    cols = jnp.where(valid, cols_ref[...], 900).astype(F32)
    rows_t = jnp.transpose(jnp.broadcast_to(rows, (B, NNZ)))
    cols_t = jnp.transpose(jnp.broadcast_to(cols, (B, NNZ)))
    sub_k = lax.broadcasted_iota(jnp.int32, (NNZ, B), 0).astype(F32)
    lane_r = lax.broadcasted_iota(jnp.int32, (NNZ, B), 1).astype(F32)
    sub_kk = lax.broadcasted_iota(jnp.int32, (NNZ, NNZ), 0)
    lane_kk = lax.broadcasted_iota(jnp.int32, (NNZ, NNZ), 1)
    sub_r = lax.broadcasted_iota(jnp.int32, (B, NNZ), 0).astype(F32)
    sub_q = lax.broadcasted_iota(jnp.int32, (B, B), 0)
    lane_q = lax.broadcasted_iota(jnp.int32, (B, B), 1)

    def half_up(n):
        return ((n.astype(jnp.int32) + 1) >> 1).astype(F32)

    def one(key, key_t, src_t, blk, src, keep, end, has):
        key_tt = jnp.concatenate([key_t] * (NNZ // B), axis=1)
        same = (key_tt == jnp.broadcast_to(key, (NNZ, NNZ))) & (sub_kk < lane_kk)
        within = jnp.sum(jnp.where(same, 1.0, 0.0), axis=0, keepdims=True)
        n_l = jnp.sum(jnp.where(key_t == lane_r, 1.0, 0.0), axis=0, keepdims=True)
        hot = jnp.where(sub_r == jnp.broadcast_to(key, (B, NNZ)), 1.0, 0.0)
        n_s = jnp.sum(hot, axis=1, keepdims=True)
        q_l = half_up(n_l)
        q_s = half_up(n_s)
        s_l = jnp.sum(jnp.where(sub_q < lane_q, jnp.broadcast_to(q_s, (B, B)), 0.0), axis=0, keepdims=True)
        s_s = jnp.sum(jnp.where(lane_q < sub_q, jnp.broadcast_to(q_l, (B, B)), 0.0), axis=1, keepdims=True)
        slot = 2.0 * jnp.sum(hot * s_s, axis=0, keepdims=True) + within
        slot = jnp.where(valid, slot, 9000.0)
        slot_t = jnp.transpose(jnp.broadcast_to(slot, (B, NNZ)))
        src_clean = jnp.where(src_t < 800.0, src_t, 0.0)
        for part in range(SLOTS // B):
            match = slot_t == lane_r + float(part * B)
            found = jnp.sum(jnp.where(match, sub_k + 1.0, 0.0), axis=0, keepdims=True)
            where = jnp.sum(jnp.where(match, src_clean, 0.0), axis=0, keepdims=True)
            found = jnp.where(found == 0.0, float(NNZ + 1), found) - 1.0
            blk[:, pl.ds(part * B, B)] = found.astype(jnp.int32)
            src[:, pl.ds(part * B, B)] = where.astype(jnp.int32)
        for part in range(2):
            first = (s_s == (lane_q + part * B).astype(F32)) & (n_s > 0.0)
            starts = jnp.sum(jnp.where(first, 1.0, 0.0), axis=0, keepdims=True)
            keep[:, pl.ds(part * B, B)] = (1.0 - starts).astype(jnp.int32)
        ends = jnp.where(n_l > 0.0, s_l + q_l - 1.0, 0.0)
        end[...] = ends.astype(jnp.int32)
        has[...] = jnp.where(n_l > 0.0, 1.0, 0.0).astype(jnp.int32)

    one(rows, rows_t, cols_t, blk_f, src_f, keep_f, end_f, has_f)
    one(cols, cols_t, rows_t, blk_b, src_b, keep_b, end_b, has_b)


def build_meta(block_rows, block_cols, counts):
    shapes = [(1, SLOTS), (1, SLOTS), (1, 2 * B), (1, B), (1, B)] * 2
    return pl.pallas_call(
        meta_kernel,
        out_shape=[jax.ShapeDtypeStruct(shape, jnp.int32) for shape in shapes],
        in_specs=[
            pl.BlockSpec(memory_space=pltpu.VMEM),
            pl.BlockSpec(memory_space=pltpu.VMEM),
            pl.BlockSpec(memory_space=pltpu.SMEM),
        ],
        out_specs=[pl.BlockSpec(memory_space=pltpu.VMEM)] * 10,
    )(block_rows, block_cols, counts)


class Ring:
    def __init__(self, i, j, slot, device):
        self.i, self.j, self.slot, self.device = i, j, slot, device

    def at(self, di, dj):
        i = (self.i + di + 4) % 4
        j = self.j if dj == 0 else 1 - self.j
        return self.slot(i, j)

    def dev(self, di, dj):
        i = (self.i + di + 4) % 4
        j = self.j if dj == 0 else 1 - self.j
        return self.device(i, j)


def remote(src, dst, send, recv, index, device):
    return pltpu.make_async_remote_copy(
        src_ref=src, dst_ref=dst, send_sem=send.at[index], recv_sem=recv.at[index], device_id=device, device_id_type=MESH
    )


def gather_steps(buf, ring, send, recv, arrived):
    def part(slot, half):
        return buf.at[pl.ds(slot * CHUNK + 2 * half, 2)]

    right, left, mate = ring.dev(1, 0), ring.dev(-1, 0), ring.dev(0, 1)
    started = []

    def go(index, slot, half, device):
        copy = remote(part(slot, half), part(slot, half), send, recv, index, device)
        copy.start()
        started.append(copy)

    def come(index, slot, half):
        remote(part(slot, half), part(slot, half), send, recv, index, right).wait_recv()
        arrived(slot, half)

    own, other = ring.at(0, 0), ring.at(0, 1)
    go(0, own, 0, mate)
    go(2, own, 0, right)
    go(8, own, 1, left)
    go(1, own, 1, mate)
    go(3, own, 1, right)
    go(9, own, 0, left)
    arrived(own, 0)
    arrived(own, 1)
    yield
    come(2, ring.at(-1, 0), 0)
    go(6, ring.at(-1, 0), 0, right)
    yield
    come(8, ring.at(1, 0), 1)
    go(12, ring.at(1, 0), 1, left)
    yield
    come(0, other, 0)
    go(4, other, 0, right)
    go(11, other, 0, left)
    yield
    come(1, other, 1)
    go(10, other, 1, left)
    go(5, other, 1, right)
    yield
    come(3, ring.at(-1, 0), 1)
    come(9, ring.at(1, 0), 0)
    yield
    come(4, ring.at(-1, 1), 0)
    go(7, ring.at(-1, 1), 0, right)
    yield
    come(10, ring.at(1, 1), 1)
    go(13, ring.at(1, 1), 1, left)
    yield
    come(6, ring.at(-2, 0), 0)
    come(12, ring.at(2, 0), 1)
    yield
    come(5, ring.at(-1, 1), 1)
    come(11, ring.at(1, 1), 0)
    yield
    come(7, ring.at(-2, 1), 0)
    come(13, ring.at(2, 1), 1)
    for copy in started:
        copy.wait_send()


def scatter_steps(buf, ring, send, recv, relay_l, relay_r, from_l, from_r, from_mate, ready, finish):
    right, left, mate = ring.dev(1, 0), ring.dev(-1, 0), ring.dev(0, 1)
    started = []

    def part(slot, half):
        return buf.at[pl.ds(slot * CHUNK + 2 * half, 2)]

    def go(index, src, dst, device):
        copy = remote(src, dst, send, recv, index, device)
        copy.start()
        started.append(copy)

    def come(index, ref):
        remote(ref, ref, send, recv, index, right).wait_recv()

    def add(slot, half, ref):
        view = part(slot, half)
        for b in range(2):
            view[b] = (view[b].astype(F32) + ref[b].astype(F32)).astype(BF)

    for dj in (1, 0):
        ready(2, dj)
        slot = ring.at(2, dj)
        go(0 + dj, part(slot, 0), relay_l.at[dj], right)
        go(2 + dj, part(slot, 1), relay_r.at[dj], left)
        yield
    for dj in (1, 0):
        ready(1, dj)
        go(4 + dj, part(ring.at(1, dj), 1), from_l.at[dj, pl.ds(2, 2)], right)
        yield
        ready(-1, dj)
        go(6 + dj, part(ring.at(-1, dj), 0), from_r.at[dj, pl.ds(0, 2)], left)
        yield
    for dj in (1, 0):
        come(0 + dj, relay_l.at[dj])
        add(ring.at(1, dj), 0, relay_l.at[dj])
        go(8 + dj, part(ring.at(1, dj), 0), from_l.at[dj, pl.ds(0, 2)], right)
        yield
        come(2 + dj, relay_r.at[dj])
        add(ring.at(-1, dj), 1, relay_r.at[dj])
        go(10 + dj, part(ring.at(-1, dj), 1), from_r.at[dj, pl.ds(2, 2)], left)
        yield
    ready(0, 1)
    ready(0, 0)
    yield
    for dj in (1, 0):
        slot = ring.at(0, dj)
        for half in range(2):
            piece = pl.ds(2 * half, 2)
            come((8 if half == 0 else 4) + dj, from_l.at[dj, piece])
            come((6 if half == 0 else 10) + dj, from_r.at[dj, piece])
            view = part(slot, half)
            for b in range(2):
                total = (
                    view[b].astype(F32)
                    + from_l[dj, 2 * half + b].astype(F32)
                    + from_r[dj, 2 * half + b].astype(F32)
                )
                if dj == 1:
                    view[b] = total.astype(BF)
                else:
                    finish(2 * half + b, total, None)
            if dj == 1:
                go(12 + half, part(slot, half), from_mate.at[piece], mate)
            yield
    for half in range(2):
        piece = pl.ds(2 * half, 2)
        come(12 + half, from_mate.at[piece])
        for b in range(2):
            finish(2 * half + b, None, from_mate[2 * half + b].astype(F32))
        yield
    for copy in started:
        copy.wait_send()


def drain(steps, times=None):
    if times is None:
        for _ in steps:
            pass
        return
    for _ in range(times):
        next(steps, None)


def fused_kernel(
    n_row, n_col, scale,
    blk_f, src_f, keep_f, end_f, has_f, blk_b, src_b, keep_b, end_b, has_b,
    features, weight, cotangent, values,
    out_ref, gw_ref, gf_ref,
    vbuf, panel, slab, stage, acc, aggbuf, gfbuf, sib_in,
    relay_l, relay_r, from_l, from_r, from_mate,
    crelay_l, crelay_r, cfrom_l, cfrom_r, cfrom_mate,
    agg32, gf32, wterm, wsum, w1, w2,
    local_sem, agc_s, agc_r, agr_s, agr_r, sib_s, sib_r, rsc_s, rsc_r, rsr_s, rsr_r, sx_s, sx_r,
    ws1_s, ws1_r, ws2_s, ws2_r, ws3_s, ws3_r,
):
    row = lax.axis_index("row")
    col = lax.axis_index("col")
    core, yl, x = row % 2, (row // 2) % 2, row // 4
    z, yh = col % 4, col // 4
    sibling = {"row": x * 4 + yl * 2 + (1 - core), "col": col}

    load_values = pltpu.make_async_copy(values, vbuf.at[pl.ds(0, NNZ)], local_sem.at[0])
    load_values.start()
    load_own = pltpu.make_async_copy(features, panel.at[pl.ds(col * CHUNK, CHUNK)], local_sem.at[1])
    load_own.start()

    barrier = pltpu.get_barrier_semaphore()

    @pl.loop(1, n_row)
    def _(d):
        pl.semaphore_signal(barrier, inc=1, device_id={"row": (row + d) % n_row, "col": col}, device_id_type=MESH)

    @pl.loop(1, n_col)
    def _(d):
        pl.semaphore_signal(barrier, inc=1, device_id={"row": row, "col": (col + d) % n_col}, device_id_type=MESH)

    vbuf[NNZ] = jnp.zeros((B, B), BF)
    for b in range(CHUNK):
        slab[row * CHUNK + b] = lax.dot_general(
            cotangent[b], weight[...], (((1,), (1,)), ((), ())), preferred_element_type=F32
        ).astype(BF)
    load_own.wait()
    pl.semaphore_wait(barrier, n_row + n_col - 2)

    ring_c = Ring(z, yh, lambda i, j: j * 4 + i, lambda i, j: {"row": row, "col": j * 4 + i})
    ring_r = Ring(
        x, yl, lambda i, j: i * 4 + j * 2 + core, lambda i, j: {"row": i * 4 + j * 2 + core, "col": col}
    )

    sib_started = []

    def to_sibling(slot, half):
        index = len(sib_started)
        ref = slab.at[pl.ds(slot * CHUNK + 2 * half, 2)]
        copy = remote(ref, ref, sib_s, sib_r, index, sibling)
        copy.start()
        sib_started.append((slot, half, copy))

    ag_c = gather_steps(panel, ring_c, agc_s, agc_r, lambda slot, half: None)
    ag_r = gather_steps(slab, ring_r, agr_s, agr_r, to_sibling)
    done = object()
    next(ag_c)
    next(ag_r)
    for _ in range(12):
        next(ag_c, done)
        next(ag_r, done)
    drain(ag_c)
    drain(ag_r)
    load_values.wait()
    for slot, half, copy in sib_started:
        theirs = slot + 1 - 2 * core
        ref = slab.at[pl.ds(theirs * CHUNK + 2 * half, 2)]
        index = [k for k, item in enumerate(sib_started) if item[2] is copy][0]
        remote(ref, ref, sib_s, sib_r, index, sibling).wait_recv()
        copy.wait_send()

    acc[...] = jnp.zeros_like(acc)

    def forward(t, _):
        a, b = blk_f[0, 2 * t], blk_f[0, 2 * t + 1]
        ca, cb = src_f[0, 2 * t], src_f[0, 2 * t + 1]
        keep = keep_f[0, t].astype(F32)
        left = jnp.concatenate([vbuf[a], vbuf[b]], axis=1)
        rhs = jnp.concatenate([panel[ca], panel[cb]], axis=0)
        total = acc[...] * keep + jnp.dot(left, rhs, preferred_element_type=F32)
        acc[...] = total
        stage[t] = total.astype(BF)
        return 0

    def backward(t, _):
        a, b = blk_b[0, 2 * t], blk_b[0, 2 * t + 1]
        ra, rb = src_b[0, 2 * t], src_b[0, 2 * t + 1]
        keep = keep_b[0, t].astype(F32)
        left = jnp.concatenate([vbuf[a], vbuf[b]], axis=0)
        rhs = jnp.concatenate([slab[ra], slab[rb]], axis=0)
        total = acc[...] * keep + lax.dot_general(
            left, rhs, (((0,), (0,)), ((), ())), preferred_element_type=F32
        )
        acc[...] = total
        stage[t] = total.astype(BF)
        return 0

    lax.fori_loop(0, F_PAIRS, forward, 0)

    def pick(target, slot, end, has):
        for b in range(CHUNK):
            r = slot * CHUNK + b
            target[r] = stage[end[0, r]] * has[0, r].astype(F32).astype(BF)

    order = [(2, 1), (2, 0), (1, 1), (-1, 1), (1, 0), (-1, 0), (0, 1), (0, 0)]
    swaps = []
    for m, (di, dj) in enumerate(order):
        slot = ring_r.at(di, dj) + 1 - 2 * core
        pick(aggbuf, slot, end_f, has_f)
        copy = remote(aggbuf.at[pl.ds(slot * CHUNK, CHUNK)], sib_in.at[pl.ds(m * CHUNK, CHUNK)], sx_s, sx_r, m, sibling)
        copy.start()
        swaps.append(copy)
    for di, dj in order:
        pick(aggbuf, ring_r.at(di, dj), end_f, has_f)

    def ready_r(di, dj):
        m = order.index((di, dj))
        slot = ring_r.at(di, dj)
        ref = sib_in.at[pl.ds(m * CHUNK, CHUNK)]
        remote(ref, ref, sx_s, sx_r, m, sibling).wait_recv()
        for b in range(CHUNK):
            r = slot * CHUNK + b
            aggbuf[r] = (aggbuf[r].astype(F32) + sib_in[m * CHUNK + b].astype(F32)).astype(BF)

    def finish_r(b, total, more):
        if more is None:
            agg32[b] = total
        else:
            agg32[b] = agg32[b] + more

    def finish_c(b, total, more):
        if more is None:
            gf32[b] = total
        else:
            gf_ref[b] = (gf32[b] + more).astype(BF)

    rs_r = scatter_steps(
        aggbuf, ring_r, rsr_s, rsr_r, relay_l, relay_r, from_l, from_r, from_mate, ready_r, finish_r
    )
    acc[...] = jnp.zeros_like(acc)
    cut = B_PAIRS // 8
    for piece in range(8):
        drain(rs_r, 1)
        lax.fori_loop(piece * cut, (piece + 1) * cut, backward, 0)
    rs_c = scatter_steps(
        gfbuf, ring_c, rsc_s, rsc_r, crelay_l, crelay_r, cfrom_l, cfrom_r, cfrom_mate,
        lambda di, dj: pick(gfbuf, ring_c.at(di, dj), end_b, has_b), finish_c,
    )
    for _ in range(6):
        drain(rs_c, 1)
        drain(rs_r, 1)
    drain(rs_c, 2)
    drain(rs_r)
    for copy in swaps:
        copy.wait_send()
    for b in range(CHUNK):
        aggregate = agg32[b].astype(BF)
        out_ref[b] = jnp.dot(aggregate, weight[...], preferred_element_type=F32).astype(BF)
        term = lax.dot_general(
            aggregate, cotangent[b], (((0,), (0,)), ((), ())), preferred_element_type=F32
        )
        if b == 0:
            wterm[...] = term.reshape(wterm.shape)
        else:
            wterm[...] = wterm[...] + term.reshape(wterm.shape)

    def w1_copy(d):
        target = (row + d) % n_row
        return remote(wterm.at[target], w1.at[d - 1], ws1_s, ws1_r, d - 1, {"row": target, "col": col})

    def w2_copy(d):
        target = (col + d) % n_col
        return remote(w2.at[col], w2.at[col], ws2_s, ws2_r, d - 1, {"row": row, "col": target})

    def w3_copy(d):
        target = (row + d) % n_row
        return remote(wsum.at[row], wsum.at[row], ws3_s, ws3_r, d - 1, {"row": target, "col": col})

    @pl.loop(1, n_row)
    def _(d):
        w1_copy(d).start()

    drain(rs_c, 4)
    share = wterm[row]
    for d in range(1, n_row):
        remote(w1.at[d - 1], w1.at[d - 1], ws1_s, ws1_r, d - 1, sibling).wait_recv()
        share = share + w1[d - 1]
    w2[col] = share

    @pl.loop(1, n_col)
    def _(d):
        w2_copy(d).start()

    drain(rs_c, 4)

    @pl.loop(1, n_col)
    def _(d):
        origin = (col + n_col - d) % n_col
        remote(w2.at[origin], w2.at[origin], ws2_s, ws2_r, d - 1, sibling).wait_recv()

    whole = w2[0]
    for c in range(1, n_col):
        whole = whole + w2[c]
    wsum[row] = whole * scale

    @pl.loop(1, n_row)
    def _(d):
        w3_copy(d).start()

    drain(rs_c)

    @pl.loop(1, n_row)
    def _(d):
        origin = (row + n_row - d) % n_row
        remote(wsum.at[origin], wsum.at[origin], ws3_s, ws3_r, d - 1, sibling).wait_recv()

    gw_ref[...] = wsum[...]

    @pl.loop(1, n_row)
    def _(d):
        w1_copy(d).wait_send()
        w3_copy(d).wait_send()

    @pl.loop(1, n_col)
    def _(d):
        w2_copy(d).wait_send()


def body(features, weight, cotangent, block_rows, block_cols, counts, values):
    n_row = lax.axis_size("row")
    n_col = lax.axis_size("col")
    width = features.shape[-1]
    nodes = features.shape[0] * n_row * n_col
    meta = build_meta(block_rows[0], block_cols[0], counts)
    shard = (CHUNK, B, width)

    def vm(*shape, dtype=BF):
        return pltpu.VMEM(shape, dtype)

    dma = pltpu.SemaphoreType.DMA
    wide = (B, width)
    scratch = [
        vm(NNZ + 1, B, B), vm(CHUNK * n_col, *wide), vm(CHUNK * n_row, *wide), vm(F_PAIRS, *wide),
        vm(*wide, dtype=F32), vm(CHUNK * n_row, *wide), vm(CHUNK * n_col, *wide), vm(CHUNK * n_row // 2, *wide),
        vm(2, 2, *wide), vm(2, 2, *wide), vm(2, CHUNK, *wide), vm(2, CHUNK, *wide), vm(*shard),
        vm(2, 2, *wide), vm(2, 2, *wide), vm(2, CHUNK, *wide), vm(2, CHUNK, *wide), vm(*shard),
        vm(*shard, dtype=F32), vm(*shard, dtype=F32),
        vm(n_row, width // n_row, width, dtype=F32), vm(n_row, width // n_row, width, dtype=F32),
        vm(n_row - 1, width // n_row, width, dtype=F32), vm(n_col, width // n_row, width, dtype=F32),
        dma((2,)), dma((14,)), dma((14,)), dma((14,)), dma((14,)), dma((16,)), dma((16,)),
        dma((14,)), dma((14,)), dma((14,)), dma((14,)), dma((8,)), dma((8,)),
        dma((n_row - 1,)), dma((n_row - 1,)), dma((n_col - 1,)), dma((n_col - 1,)), dma((n_row - 1,)), dma((n_row - 1,)),
    ]
    vmem = pl.BlockSpec(memory_space=pltpu.VMEM)
    out, gw, gf = pl.pallas_call(
        functools.partial(fused_kernel, n_row, n_col, float(nodes) ** -0.5),
        out_shape=[
            jax.ShapeDtypeStruct(shard, BF),
            jax.ShapeDtypeStruct((n_row, width // n_row, width), F32),
            jax.ShapeDtypeStruct(shard, BF),
        ],
        in_specs=[pl.BlockSpec(memory_space=pltpu.SMEM)] * 10
        + [pl.BlockSpec(memory_space=pl.ANY), vmem, vmem, pl.BlockSpec(memory_space=pl.ANY)],
        out_specs=[vmem] * 3,
        scratch_shapes=scratch,
        compiler_params=pltpu.CompilerParams(
            collective_id=0, has_side_effects=True, vmem_limit_bytes=60 * 1024 * 1024
        ),
    )(*meta, features.reshape(shard), weight, cotangent.reshape(shard), values[0, 0])
    return out.reshape(features.shape), gw.reshape(width, width), gf.reshape(features.shape)


def solution(mesh):
    placed = (
        P(("row", "col"), None),
        P(),
        P(("col", "row"), None),
        P("row", "col", None),
        P("row", "col", None),
        P("row", "col"),
        P("row", "col", None, None, None),
    )
    return jax.shard_map(
        body,
        mesh=mesh,
        in_specs=placed,
        out_specs=(P(("col", "row"), None), P(), P(("row", "col"), None)),
        check_vma=False,
    )
```

```python
import functools

import jax
import jax.numpy as jnp
from jax import lax
from jax.experimental import pallas as pl
from jax.experimental.pallas import tpu as pltpu
from jax.sharding import PartitionSpec as P

MESH = pl.DeviceIdType.MESH
BF = jnp.bfloat16
F32 = jnp.float32
B = 128
NNZ = 384
SLOTS = 512
F_PAIRS = 224
B_PAIRS = 208
CHUNK = 4
UNROLL = 16
BLK, SRC, KEEP, END, HAS, META = 0, 512, 1024, 1280, 1408, 1536


def meta_kernel(rows_ref, cols_ref, count_ref, meta):
    count = count_ref[0, 0]
    lane_k = lax.broadcasted_iota(jnp.int32, (1, NNZ), 1)
    valid = lane_k < count
    rows = jnp.where(valid, rows_ref[...], 900).astype(F32)
    cols = jnp.where(valid, cols_ref[...], 900).astype(F32)
    rows_t = jnp.transpose(jnp.broadcast_to(rows, (B, NNZ)))
    cols_t = jnp.transpose(jnp.broadcast_to(cols, (B, NNZ)))
    sub_k = lax.broadcasted_iota(jnp.int32, (NNZ, B), 0).astype(F32)
    lane_r = lax.broadcasted_iota(jnp.int32, (NNZ, B), 1).astype(F32)
    sub_kk = lax.broadcasted_iota(jnp.int32, (NNZ, NNZ), 0)
    lane_kk = lax.broadcasted_iota(jnp.int32, (NNZ, NNZ), 1)
    sub_r = lax.broadcasted_iota(jnp.int32, (B, NNZ), 0).astype(F32)
    sub_q = lax.broadcasted_iota(jnp.int32, (B, B), 0)
    lane_q = lax.broadcasted_iota(jnp.int32, (B, B), 1)

    def half_up(n):
        return ((n.astype(jnp.int32) + 1) >> 1).astype(F32)

    def one(key, key_t, src_t, base):
        key_tt = jnp.concatenate([key_t] * (NNZ // B), axis=1)
        same = (key_tt == jnp.broadcast_to(key, (NNZ, NNZ))) & (sub_kk < lane_kk)
        within = jnp.sum(jnp.where(same, 1.0, 0.0), axis=0, keepdims=True)
        n_l = jnp.sum(jnp.where(key_t == lane_r, 1.0, 0.0), axis=0, keepdims=True)
        hot = jnp.where(sub_r == jnp.broadcast_to(key, (B, NNZ)), 1.0, 0.0)
        n_s = jnp.sum(hot, axis=1, keepdims=True)
        q_l = half_up(n_l)
        q_s = half_up(n_s)
        s_l = jnp.sum(jnp.where(sub_q < lane_q, jnp.broadcast_to(q_s, (B, B)), 0.0), axis=0, keepdims=True)
        s_s = jnp.sum(jnp.where(lane_q < sub_q, jnp.broadcast_to(q_l, (B, B)), 0.0), axis=1, keepdims=True)
        slot = 2.0 * jnp.sum(hot * s_s, axis=0, keepdims=True) + within
        slot = jnp.where(valid, slot, 9000.0)
        slot_t = jnp.transpose(jnp.broadcast_to(slot, (B, NNZ)))
        src_clean = jnp.where(src_t < 800.0, src_t, 0.0)
        for part in range(SLOTS // B):
            match = slot_t == lane_r + float(part * B)
            found = jnp.sum(jnp.where(match, sub_k + 1.0, 0.0), axis=0, keepdims=True)
            where = jnp.sum(jnp.where(match, src_clean, 0.0), axis=0, keepdims=True)
            found = jnp.where(found == 0.0, float(NNZ + 1), found) - 1.0
            meta[:, pl.ds(base + BLK + part * B, B)] = found.astype(jnp.int32)
            meta[:, pl.ds(base + SRC + part * B, B)] = where.astype(jnp.int32)
        for part in range(2):
            first = (s_s == (lane_q + part * B).astype(F32)) & (n_s > 0.0)
            starts = jnp.sum(jnp.where(first, 1.0, 0.0), axis=0, keepdims=True)
            meta[:, pl.ds(base + KEEP + part * B, B)] = (1.0 - starts).astype(jnp.int32)
        ends = jnp.where(n_l > 0.0, s_l + q_l - 1.0, 0.0)
        meta[:, pl.ds(base + END, B)] = ends.astype(jnp.int32)
        meta[:, pl.ds(base + HAS, B)] = jnp.where(n_l > 0.0, 1.0, 0.0).astype(jnp.int32)

    one(rows, rows_t, cols_t, 0)
    one(cols, cols_t, rows_t, META)


def build_meta(block_rows, block_cols, counts):
    return pl.pallas_call(
        meta_kernel,
        out_shape=jax.ShapeDtypeStruct((1, 2 * META), jnp.int32),
        in_specs=[
            pl.BlockSpec(memory_space=pltpu.VMEM),
            pl.BlockSpec(memory_space=pltpu.VMEM),
            pl.BlockSpec(memory_space=pltpu.SMEM),
        ],
        out_specs=pl.BlockSpec(memory_space=pltpu.VMEM),
    )(block_rows, block_cols, counts)


def hand_over(src_a, src_b, src_c, dst_a, dst_b, dst_c):
    dst_a[...] = src_a[...]
    dst_b[...] = src_b[...]
    dst_c[...] = src_c[...]


class Ring:
    def __init__(self, i, j, slot, device):
        self.i, self.j, self.slot, self.device = i, j, slot, device

    def at(self, di, dj):
        i = (self.i + di + 4) % 4
        j = self.j if dj == 0 else 1 - self.j
        return self.slot(i, j)

    def dev(self, di, dj):
        i = (self.i + di + 4) % 4
        j = self.j if dj == 0 else 1 - self.j
        return self.device(i, j)


def remote(src, dst, send, recv, index, device):
    return pltpu.make_async_remote_copy(
        src_ref=src, dst_ref=dst, send_sem=send.at[index], recv_sem=recv.at[index], device_id=device, device_id_type=MESH
    )


def gather_steps(buf, ring, send, recv, arrived, pair_first):
    def part(slot, half):
        return buf.at[pl.ds(slot * CHUNK + 2 * half, 2)]

    right, left, mate = ring.dev(1, 0), ring.dev(-1, 0), ring.dev(0, 1)
    started = []

    def go(index, slot, half, device):
        copy = remote(part(slot, half), part(slot, half), send, recv, index, device)
        copy.start()
        started.append(copy)

    def come(index, slot, half):
        remote(part(slot, half), part(slot, half), send, recv, index, right).wait_recv()
        arrived(slot, half)

    own, other = ring.at(0, 0), ring.at(0, 1)
    if pair_first:
        go(0, own, 0, mate)
    go(2, own, 0, right)
    go(8, own, 1, left)
    if pair_first:
        go(1, own, 1, mate)
    go(3, own, 1, right)
    go(9, own, 0, left)
    arrived(own, 0)
    arrived(own, 1)
    yield
    come(2, ring.at(-1, 0), 0)
    go(6, ring.at(-1, 0), 0, right)
    if not pair_first:
        go(0, own, 0, mate)
        go(1, own, 1, mate)
    yield
    come(8, ring.at(1, 0), 1)
    go(12, ring.at(1, 0), 1, left)
    yield
    come(0, other, 0)
    go(4, other, 0, right)
    go(11, other, 0, left)
    yield
    come(1, other, 1)
    go(10, other, 1, left)
    go(5, other, 1, right)
    yield
    come(3, ring.at(-1, 0), 1)
    come(9, ring.at(1, 0), 0)
    yield
    come(4, ring.at(-1, 1), 0)
    go(7, ring.at(-1, 1), 0, right)
    yield
    come(10, ring.at(1, 1), 1)
    go(13, ring.at(1, 1), 1, left)
    yield
    come(6, ring.at(-2, 0), 0)
    come(12, ring.at(2, 0), 1)
    yield
    come(5, ring.at(-1, 1), 1)
    come(11, ring.at(1, 1), 0)
    yield
    come(7, ring.at(-2, 1), 0)
    come(13, ring.at(2, 1), 1)
    for copy in started:
        copy.wait_send()


def scatter_steps(buf, ring, send, recv, relay_l, relay_r, from_l, from_r, from_mate, ready, after, finish):
    right, left, mate = ring.dev(1, 0), ring.dev(-1, 0), ring.dev(0, 1)
    started = []

    def part(slot, half):
        return buf.at[pl.ds(slot * CHUNK + 2 * half, 2)]

    def go(index, src, dst, device):
        copy = remote(src, dst, send, recv, index, device)
        copy.start()
        started.append(copy)

    def come(index, ref):
        remote(ref, ref, send, recv, index, right).wait_recv()

    def add(slot, half, ref):
        view = part(slot, half)
        for b in range(2):
            view[b] = (view[b].astype(F32) + ref[b].astype(F32)).astype(BF)

    def feed(dj):
        ready(2, dj)
        slot = ring.at(2, dj)
        go(0 + dj, part(slot, 0), relay_l.at[dj], right)
        go(2 + dj, part(slot, 1), relay_r.at[dj], left)
        after(2, dj)
        yield
        ready(1, dj)
        go(4 + dj, part(ring.at(1, dj), 1), from_l.at[dj, pl.ds(2, 2)], right)
        after(1, dj)
        yield
        ready(-1, dj)
        go(6 + dj, part(ring.at(-1, dj), 0), from_r.at[dj, pl.ds(0, 2)], left)
        after(-1, dj)
        yield

    def relay(dj):
        come(0 + dj, relay_l.at[dj])
        add(ring.at(1, dj), 0, relay_l.at[dj])
        go(8 + dj, part(ring.at(1, dj), 0), from_l.at[dj, pl.ds(0, 2)], right)
        yield
        come(2 + dj, relay_r.at[dj])
        add(ring.at(-1, dj), 1, relay_r.at[dj])
        go(10 + dj, part(ring.at(-1, dj), 1), from_r.at[dj, pl.ds(2, 2)], left)
        yield

    def landed(dj, half):
        piece = pl.ds(2 * half, 2)
        come((8 if half == 0 else 4) + dj, from_l.at[dj, piece])
        come((6 if half == 0 else 10) + dj, from_r.at[dj, piece])

    def total(dj, k):
        r = ring.at(0, dj) * CHUNK + k
        return buf[r].astype(F32) + from_l[dj, k].astype(F32) + from_r[dj, k].astype(F32)

    yield from feed(1)
    yield from relay(1)
    yield from feed(0)
    for dj in (1, 0):
        ready(0, dj)
        after(0, dj)
    yield
    for half in range(2):
        landed(1, half)
        for k in (2 * half, 2 * half + 1):
            buf[ring.at(0, 1) * CHUNK + k] = total(1, k).astype(BF)
        go(12 + half, part(ring.at(0, 1), half), from_mate.at[pl.ds(2 * half, 2)], mate)
    yield
    yield from relay(0)
    for half in range(2):
        landed(0, half)
        come(12 + half, from_mate.at[pl.ds(2 * half, 2)])
        for k in (2 * half, 2 * half + 1):
            finish(k, total(0, k) + from_mate[k].astype(F32))
    for copy in started:
        copy.wait_send()


def drain(steps, times=None):
    if times is None:
        for _ in steps:
            pass
        return
    for _ in range(times):
        next(steps, None)


def fused_kernel(
    n_row, n_col, scale,
    meta, features, weight, cotangent, values,
    out_ref, gw_ref, gf_ref,
    vbuf, panel, cslab, slab, stage, acc, aggbuf, gfbuf, sib_in,
    relay_l, relay_r, from_l, from_r, from_mate,
    crelay_l, crelay_r, cfrom_l, cfrom_r, cfrom_mate,
    agg, wterm, wsum, w1, w2, whalf,
    local_sem, agc_s, agc_r, agr_s, agr_r, sib_s, sib_r, rsc_s, rsc_r, rsr_s, rsr_r, sx_s, sx_r,
    ws1_s, ws1_r, ws2_s, ws2_r, ws3_s, ws3_r, wc_s, wc_r,
):
    row = lax.axis_index("row")
    col = lax.axis_index("col")
    core, yl, x = row % 2, (row // 2) % 2, row // 4
    z, yh = col % 4, col // 4
    sibling = {"row": x * 4 + yl * 2 + (1 - core), "col": col}

    load_values = pltpu.make_async_copy(values, vbuf.at[pl.ds(0, NNZ)], local_sem.at[0])
    load_values.start()
    load_own = pltpu.make_async_copy(features, panel.at[pl.ds(col * CHUNK, CHUNK)], local_sem.at[1])
    load_own.start()
    load_cot = pltpu.make_async_copy(cotangent, cslab.at[pl.ds(row * CHUNK, CHUNK)], local_sem.at[2])
    load_cot.start()

    barrier = pltpu.get_barrier_semaphore()

    @pl.loop(1, n_row)
    def _(d):
        pl.semaphore_signal(barrier, inc=1, device_id={"row": (row + d) % n_row, "col": col}, device_id_type=MESH)

    @pl.loop(1, n_col)
    def _(d):
        pl.semaphore_signal(barrier, inc=1, device_id={"row": row, "col": (col + d) % n_col}, device_id_type=MESH)

    vbuf[NNZ] = jnp.zeros((B, B), BF)
    load_own.wait()
    load_cot.wait()
    pl.semaphore_wait(barrier, n_row + n_col - 2)

    ring_c = Ring(z, yh, lambda i, j: j * 4 + i, lambda i, j: {"row": row, "col": j * 4 + i})
    ring_r = Ring(
        x, yl, lambda i, j: i * 4 + j * 2 + core, lambda i, j: {"row": i * 4 + j * 2 + core, "col": col}
    )

    sib_started = []
    sib_taken = []

    def backprop(slot, half):
        piece = pl.ds(slot * CHUNK + 2 * half, 2)
        rows = cslab[piece].reshape(2 * B, cslab.shape[-1])
        grad = lax.dot_general(rows, weight[...], (((1,), (1,)), ((), ())), preferred_element_type=F32)
        slab[piece] = grad.astype(BF).reshape(2, B, cslab.shape[-1])

    def from_sibling(upto):
        while len(sib_taken) < upto:
            index = len(sib_taken)
            slot, half, copy = sib_started[index]
            theirs = slot + 1 - 2 * core
            ref = cslab.at[pl.ds(theirs * CHUNK + 2 * half, 2)]
            remote(ref, ref, sib_s, sib_r, index, sibling).wait_recv()
            backprop(theirs, half)
            sib_taken.append(copy)

    def to_sibling(slot, half):
        index = len(sib_started)
        ref = cslab.at[pl.ds(slot * CHUNK + 2 * half, 2)]
        copy = remote(ref, ref, sib_s, sib_r, index, sibling)
        copy.start()
        backprop(slot, half)
        from_sibling(index - 2)
        sib_started.append((slot, half, copy))

    ag_c = gather_steps(panel, ring_c, agc_s, agc_r, lambda slot, half: None, True)
    ag_r = gather_steps(cslab, ring_r, agr_s, agr_r, to_sibling, False)
    done = object()
    next(ag_c)
    next(ag_r)
    for index in range(9):
        next(ag_c, done)
        if index >= 1:
            next(ag_r, done)
    drain(ag_c)
    load_values.wait()
    acc[...] = jnp.zeros_like(acc)
    def forward(t, _):
        a, b = meta[0, BLK + 2 * t], meta[0, BLK + 2 * t + 1]
        ca, cb = meta[0, SRC + 2 * t], meta[0, SRC + 2 * t + 1]
        keep = meta[0, KEEP + t].astype(F32)
        left = jnp.concatenate([vbuf[a], vbuf[b]], axis=1)
        rhs = jnp.concatenate([panel[ca], panel[cb]], axis=0)
        total = acc[...] * keep + jnp.dot(left, rhs, preferred_element_type=F32)
        acc[...] = total
        stage[t] = total.astype(BF)
        return 0

    def backward(t, _):
        a, b = meta[0, META + BLK + 2 * t], meta[0, META + BLK + 2 * t + 1]
        ra, rb = meta[0, META + SRC + 2 * t], meta[0, META + SRC + 2 * t + 1]
        keep = meta[0, META + KEEP + t].astype(F32)
        left = jnp.concatenate([vbuf[a], vbuf[b]], axis=0)
        rhs = jnp.concatenate([slab[ra], slab[rb]], axis=0)
        total = acc[...] * keep + lax.dot_general(
            left, rhs, (((0,), (0,)), ((), ())), preferred_element_type=F32
        )
        acc[...] = total
        stage[t] = total.astype(BF)
        return 0

    f_cut = F_PAIRS // 7
    for piece in range(7):
        lax.fori_loop(piece * f_cut, (piece + 1) * f_cut, forward, 0, unroll=UNROLL)
        next(ag_r, done)
    drain(ag_r)

    def pick(target, slot, base):
        for b in range(CHUNK):
            r = slot * CHUNK + b
            target[r] = stage[meta[0, base + END + r]] * meta[0, base + HAS + r].astype(F32).astype(BF)

    order = [(2, 1), (1, 1), (-1, 1), (2, 0), (1, 0), (-1, 0), (0, 1), (0, 0)]
    swaps = []
    for m, (di, dj) in enumerate(order):
        slot = ring_r.at(di, dj) + 1 - 2 * core
        pick(aggbuf, slot, 0)
        copy = remote(aggbuf.at[pl.ds(slot * CHUNK, CHUNK)], sib_in.at[pl.ds(m * CHUNK, CHUNK)], sx_s, sx_r, m, sibling)
        copy.start()
        swaps.append(copy)
    for di, dj in order:
        pick(aggbuf, ring_r.at(di, dj), 0)

    def ready_r(di, dj):
        m = order.index((di, dj))
        slot = ring_r.at(di, dj)
        ref = sib_in.at[pl.ds(m * CHUNK, CHUNK)]
        remote(ref, ref, sx_s, sx_r, m, sibling).wait_recv()
        for b in range(CHUNK):
            r = slot * CHUNK + b
            aggbuf[r] = (aggbuf[r].astype(F32) + sib_in[m * CHUNK + b].astype(F32)).astype(BF)

    seen = []

    def after_r(di, dj):
        piece = pl.ds(ring_r.at(di, dj) * CHUNK, CHUNK)
        width = aggbuf.shape[-1]
        term = lax.dot_general(
            aggbuf[piece].reshape(CHUNK * B, width), cslab[piece].reshape(CHUNK * B, width),
            (((0,), (0,)), ((), ())), preferred_element_type=F32,
        ).reshape(wterm.shape)
        wterm[...] = wterm[...] + term if seen else term
        seen.append((di, dj))

    def finish_r(k, total):
        agg[k] = total.astype(BF)

    def finish_c(k, total):
        gf_ref[k] = total.astype(BF)

    rs_r = scatter_steps(
        aggbuf, ring_r, rsr_s, rsr_r, relay_l, relay_r, from_l, from_r, from_mate, ready_r, after_r, finish_r
    )
    acc[...] = jnp.zeros_like(acc)
    from_sibling(16)
    for copy in sib_taken:
        copy.wait_send()
    for piece in range(13):
        lax.fori_loop(piece * UNROLL, (piece + 1) * UNROLL, backward, 0, unroll=UNROLL)
        if piece in (0, 1, 2, 6, 7, 8, 9, 10, 12):
            drain(rs_r, 1)
    rs_c = scatter_steps(
        gfbuf, ring_c, rsc_s, rsc_r, crelay_l, crelay_r, cfrom_l, cfrom_r, cfrom_mate,
        lambda di, dj: pick(gfbuf, ring_c.at(di, dj), META), lambda di, dj: None, finish_c,
    )
    spot = x * 2 + yl
    n_chip = n_row // 2

    def chip(d):
        other = (spot + d) % n_chip
        return other, {"row": other * 2 + core, "col": col}

    def w1_copy(d):
        other, device = chip(d)
        return remote(wterm.at[core, other], w1.at[d - 1], ws1_s, ws1_r, d - 1, device)

    def w2_copy(d):
        target = (col + d) % n_col
        return remote(w2.at[col], w2.at[col], ws2_s, ws2_r, d - 1, {"row": row, "col": target})

    def w3_copy(d):
        _, device = chip(d)
        return remote(wsum.at[core, spot], wsum.at[core, spot], ws3_s, ws3_r, d - 1, device)

    drain(rs_c, 3)
    to_core = remote(wterm.at[1 - core], whalf, wc_s, wc_r, 0, sibling)
    to_core.start()
    drain(rs_r, 1)
    to_core.wait_recv()
    wterm[core] = wterm[core] + whalf[...]
    for d in range(1, n_chip):
        w1_copy(d).start()
    drain(rs_c, 5)
    drain(rs_r, 2)
    share = wterm[core, spot]
    for d in range(1, n_chip):
        w1_copy(d).wait_recv()
        share = share + w1[d - 1]
    w2[col] = share
    for d in range(1, n_col):
        w2_copy(d).start()
    drain(rs_c, 2)
    drain(rs_r)
    for copy in swaps:
        copy.wait_send()
    for b in range(CHUNK):
        out_ref[b] = jnp.dot(agg[b], weight[...], preferred_element_type=F32).astype(BF)
    for d in range(1, n_col):
        origin = (col + n_col - d) % n_col
        remote(w2.at[origin], w2.at[origin], ws2_s, ws2_r, d - 1, sibling).wait_recv()
    whole = w2[0]
    for c in range(1, n_col):
        whole = whole + w2[c]
    wsum[core, spot] = whole * scale
    for d in range(1, n_chip):
        w3_copy(d).start()
    drain(rs_c, 2)
    for d in range(1, n_chip):
        origin = (spot + n_chip - d) % n_chip
        remote(wsum.at[core, origin], wsum.at[core, origin], ws3_s, ws3_r, d - 1, sibling).wait_recv()
    back = remote(wsum.at[core], wsum.at[core], wc_s, wc_r, 1, sibling)
    back.start()
    drain(rs_c)
    remote(wsum.at[1 - core], wsum.at[1 - core], wc_s, wc_r, 1, sibling).wait_recv()
    gw_ref[...] = wsum[...]
    for d in range(1, n_chip):
        w1_copy(d).wait_send()
        w3_copy(d).wait_send()
    for d in range(1, n_col):
        w2_copy(d).wait_send()
    to_core.wait_send()
    back.wait_send()


def body(features, weight, cotangent, block_rows, block_cols, counts, values):
    n_row = lax.axis_size("row")
    n_col = lax.axis_size("col")
    width = features.shape[-1]
    nodes = features.shape[0] * n_row * n_col
    meta = build_meta(block_rows[0], block_cols[0], counts)
    shard = (CHUNK, B, width)

    def vm(*shape, dtype=BF):
        return pltpu.VMEM(shape, dtype)

    dma = pltpu.SemaphoreType.DMA
    wide = (B, width)
    scratch = [
        vm(NNZ + 1, B, B), vm(CHUNK * n_col, *wide), vm(CHUNK * n_row, *wide), vm(CHUNK * n_row, *wide), vm(F_PAIRS, *wide),
        vm(*wide, dtype=F32), vm(CHUNK * n_row, *wide), vm(CHUNK * n_col, *wide), vm(CHUNK * n_row // 2, *wide),
        vm(2, 2, *wide), vm(2, 2, *wide), vm(2, CHUNK, *wide), vm(2, CHUNK, *wide), vm(*shard),
        vm(2, 2, *wide), vm(2, 2, *wide), vm(2, CHUNK, *wide), vm(2, CHUNK, *wide), vm(*shard),
        vm(*shard),
        vm(2, n_row // 2, width // n_row, width, dtype=F32), vm(2, n_row // 2, width // n_row, width, dtype=F32),
        vm(n_row // 2 - 1, width // n_row, width, dtype=F32), vm(n_col, width // n_row, width, dtype=F32),
        vm(n_row // 2, width // n_row, width, dtype=F32),
        dma((3,)), dma((14,)), dma((14,)), dma((14,)), dma((14,)), dma((16,)), dma((16,)),
        dma((14,)), dma((14,)), dma((14,)), dma((14,)), dma((8,)), dma((8,)),
        dma((n_row // 2 - 1,)), dma((n_row // 2 - 1,)), dma((n_col - 1,)), dma((n_col - 1,)),
        dma((n_row // 2 - 1,)), dma((n_row // 2 - 1,)), dma((2,)), dma((2,)),
    ]
    vmem = pl.BlockSpec(memory_space=pltpu.VMEM)
    out, gw, gf = pl.pallas_call(
        functools.partial(fused_kernel, n_row, n_col, float(nodes) ** -0.5),
        out_shape=[
            jax.ShapeDtypeStruct(shard, BF),
            jax.ShapeDtypeStruct((2, n_row // 2, width // n_row, width), F32),
            jax.ShapeDtypeStruct(shard, BF),
        ],
        in_specs=[pl.BlockSpec(memory_space=pltpu.SMEM), pl.BlockSpec(memory_space=pl.ANY), vmem] + [pl.BlockSpec(memory_space=pl.ANY)] * 2,
        out_specs=[vmem] * 3,
        scratch_shapes=scratch,
        compiler_params=pltpu.CompilerParams(
            collective_id=0, has_side_effects=True, vmem_limit_bytes=60 * 1024 * 1024
        ),
    )(meta, features.reshape(shard), weight, cotangent.reshape(shard), values[0, 0])
    out, gw, gf = pl.pallas_call(
        hand_over,
        out_shape=[jax.ShapeDtypeStruct(item.shape, item.dtype) for item in (out, gw, gf)],
        in_specs=[vmem] * 3,
        out_specs=[vmem] * 3,
    )(out, gw, gf)
    return out.reshape(features.shape), gw.reshape(width, width), gf.reshape(features.shape)


def solution(mesh):
    placed = (
        P(("row", "col"), None),
        P(),
        P(("col", "row"), None),
        P("row", "col", None),
        P("row", "col", None),
        P("row", "col"),
        P("row", "col", None, None, None),
    )
    return jax.shard_map(
        body,
        mesh=mesh,
        in_specs=placed,
        out_specs=(P(("col", "row"), None), P(), P(("row", "col"), None)),
        check_vma=False,
    )
```

```python
import functools

import jax
import jax.numpy as jnp
from jax import lax
from jax.experimental import pallas as pl
from jax.experimental.pallas import tpu as pltpu
from jax.sharding import PartitionSpec as P

MESH = pl.DeviceIdType.MESH
BF = jnp.bfloat16
F32 = jnp.float32
B = 128
NNZ = 384
SLOTS = 512
F_PAIRS = 224
B_PAIRS = 208
CHUNK = 4
UNROLL = 16
BLK, SRC, KEEP, END, HAS, META = 0, 512, 1024, 1280, 1408, 1536


def sort_blocks(rows_ref, cols_ref, count_ref, meta):
    count = count_ref[0, 0]

    def iota(shape, axis):
        return lax.broadcasted_iota(jnp.int32, shape, axis)

    valid = iota((1, NNZ), 1) < count
    rows = jnp.where(valid, rows_ref[...], 900)
    cols = jnp.where(valid, cols_ref[...], 900)
    rows_t = jnp.transpose(jnp.broadcast_to(rows, (B, NNZ)))
    cols_t = jnp.transpose(jnp.broadcast_to(cols, (B, NNZ)))
    sub_k = iota((NNZ, B), 0)
    lane_r = iota((NNZ, B), 1)
    earlier = iota((NNZ, NNZ), 0) < iota((NNZ, NNZ), 1)
    sub_r = iota((B, NNZ), 0)
    sub_q = iota((B, B), 0)
    lane_q = iota((B, B), 1)

    def count_up(mask, axis):
        return jnp.sum(jnp.where(mask, 1, 0), axis=axis, keepdims=True)

    def one(key, key_t, src_t, base):
        key_tt = jnp.concatenate([key_t] * (NNZ // B), axis=1)
        within = count_up((key_tt == jnp.broadcast_to(key, (NNZ, NNZ))) & earlier, 0)
        n_l = count_up(key_t == lane_r, 0)
        hot = sub_r == jnp.broadcast_to(key, (B, NNZ))
        n_s = count_up(hot, 1)
        q_l = (n_l + 1) >> 1
        q_s = (n_s + 1) >> 1
        s_l = jnp.sum(jnp.where(sub_q < lane_q, jnp.broadcast_to(q_s, (B, B)), 0), axis=0, keepdims=True)
        s_s = jnp.sum(jnp.where(lane_q < sub_q, jnp.broadcast_to(q_l, (B, B)), 0), axis=1, keepdims=True)
        slot = 2 * jnp.sum(jnp.where(hot, jnp.broadcast_to(s_s, (B, NNZ)), 0), axis=0, keepdims=True) + within
        slot = jnp.where(valid, slot, 9000)
        slot_t = jnp.transpose(jnp.broadcast_to(slot, (B, NNZ)))
        src_clean = jnp.where(src_t < 800, src_t, 0)
        for part in range(SLOTS // B):
            match = slot_t == lane_r + part * B
            found = jnp.sum(jnp.where(match, sub_k + 1, 0), axis=0, keepdims=True)
            where = jnp.sum(jnp.where(match, src_clean, 0), axis=0, keepdims=True)
            meta[:, pl.ds(base + BLK + part * B, B)] = jnp.where(found == 0, NNZ, found - 1)
            meta[:, pl.ds(base + SRC + part * B, B)] = where
        for part in range(2):
            first = (s_s == lane_q + part * B) & (n_s > 0)
            meta[:, pl.ds(base + KEEP + part * B, B)] = 1 - count_up(first, 0)
        meta[:, pl.ds(base + END, B)] = jnp.where(n_l > 0, s_l + q_l - 1, 0)
        meta[:, pl.ds(base + HAS, B)] = jnp.where(n_l > 0, 1, 0)

    one(rows, rows_t, cols_t, 0)
    one(cols, cols_t, rows_t, META)


def hand_over(src_a, src_b, src_c, dst_a, dst_b, dst_c):
    dst_a[...] = src_a[...]
    dst_b[...] = src_b[...]
    dst_c[...] = src_c[...]


class Ring:
    def __init__(self, i, j, slot, device):
        self.i, self.j, self.slot, self.device = i, j, slot, device

    def at(self, di, dj):
        i = (self.i + di + 4) % 4
        j = self.j if dj == 0 else 1 - self.j
        return self.slot(i, j)

    def dev(self, di, dj):
        i = (self.i + di + 4) % 4
        j = self.j if dj == 0 else 1 - self.j
        return self.device(i, j)


def remote(src, dst, send, recv, index, device):
    return pltpu.make_async_remote_copy(
        src_ref=src, dst_ref=dst, send_sem=send.at[index], recv_sem=recv.at[index], device_id=device, device_id_type=MESH
    )


def gather_steps(buf, ring, send, recv, arrived, pair_first):
    def part(slot, half):
        return buf.at[pl.ds(slot * CHUNK + 2 * half, 2)]

    right, left, mate = ring.dev(1, 0), ring.dev(-1, 0), ring.dev(0, 1)
    started = []

    def go(index, slot, half, device):
        copy = remote(part(slot, half), part(slot, half), send, recv, index, device)
        copy.start()
        started.append(copy)

    def come(index, slot, half):
        remote(part(slot, half), part(slot, half), send, recv, index, right).wait_recv()
        arrived(slot, half)

    own, other = ring.at(0, 0), ring.at(0, 1)
    if pair_first:
        go(0, own, 0, mate)
    go(2, own, 0, right)
    go(8, own, 1, left)
    if pair_first:
        go(1, own, 1, mate)
    go(3, own, 1, right)
    go(9, own, 0, left)
    arrived(own, 0)
    arrived(own, 1)
    yield
    come(2, ring.at(-1, 0), 0)
    go(6, ring.at(-1, 0), 0, right)
    if not pair_first:
        go(0, own, 0, mate)
        go(1, own, 1, mate)
    yield
    come(8, ring.at(1, 0), 1)
    go(12, ring.at(1, 0), 1, left)
    yield
    come(0, other, 0)
    go(4, other, 0, right)
    go(11, other, 0, left)
    yield
    come(1, other, 1)
    go(10, other, 1, left)
    go(5, other, 1, right)
    yield
    come(3, ring.at(-1, 0), 1)
    come(9, ring.at(1, 0), 0)
    yield
    come(4, ring.at(-1, 1), 0)
    go(7, ring.at(-1, 1), 0, right)
    yield
    come(10, ring.at(1, 1), 1)
    go(13, ring.at(1, 1), 1, left)
    yield
    come(6, ring.at(-2, 0), 0)
    come(12, ring.at(2, 0), 1)
    yield
    come(5, ring.at(-1, 1), 1)
    come(11, ring.at(1, 1), 0)
    yield
    come(7, ring.at(-2, 1), 0)
    come(13, ring.at(2, 1), 1)
    for copy in started:
        copy.wait_send()


def scatter_steps(buf, ring, send, recv, relay_l, relay_r, from_l, from_r, from_mate, ready, after, finish):
    right, left, mate = ring.dev(1, 0), ring.dev(-1, 0), ring.dev(0, 1)
    started = []

    def part(slot, half):
        return buf.at[pl.ds(slot * CHUNK + 2 * half, 2)]

    def go(index, src, dst, device):
        copy = remote(src, dst, send, recv, index, device)
        copy.start()
        started.append(copy)

    def come(index, ref):
        remote(ref, ref, send, recv, index, right).wait_recv()

    def add(slot, half, ref):
        view = part(slot, half)
        for b in range(2):
            view[b] = (view[b].astype(F32) + ref[b].astype(F32)).astype(BF)

    def feed(dj):
        ready(2, dj)
        slot = ring.at(2, dj)
        go(0 + dj, part(slot, 0), relay_l.at[dj], right)
        go(2 + dj, part(slot, 1), relay_r.at[dj], left)
        after(2, dj)
        yield
        ready(1, dj)
        go(4 + dj, part(ring.at(1, dj), 1), from_l.at[dj, pl.ds(2, 2)], right)
        after(1, dj)
        yield
        ready(-1, dj)
        go(6 + dj, part(ring.at(-1, dj), 0), from_r.at[dj, pl.ds(0, 2)], left)
        after(-1, dj)
        yield

    def relay(dj):
        come(0 + dj, relay_l.at[dj])
        add(ring.at(1, dj), 0, relay_l.at[dj])
        go(8 + dj, part(ring.at(1, dj), 0), from_l.at[dj, pl.ds(0, 2)], right)
        yield
        come(2 + dj, relay_r.at[dj])
        add(ring.at(-1, dj), 1, relay_r.at[dj])
        go(10 + dj, part(ring.at(-1, dj), 1), from_r.at[dj, pl.ds(2, 2)], left)
        yield

    def landed(dj, half):
        piece = pl.ds(2 * half, 2)
        come((8 if half == 0 else 4) + dj, from_l.at[dj, piece])
        come((6 if half == 0 else 10) + dj, from_r.at[dj, piece])

    def total(dj, k):
        r = ring.at(0, dj) * CHUNK + k
        return buf[r].astype(F32) + from_l[dj, k].astype(F32) + from_r[dj, k].astype(F32)

    yield from feed(1)
    yield from relay(1)
    yield from feed(0)
    for dj in (1, 0):
        ready(0, dj)
        after(0, dj)
    yield
    for half in range(2):
        landed(1, half)
        for k in (2 * half, 2 * half + 1):
            buf[ring.at(0, 1) * CHUNK + k] = total(1, k).astype(BF)
        go(12 + half, part(ring.at(0, 1), half), from_mate.at[pl.ds(2 * half, 2)], mate)
    yield
    yield from relay(0)
    for half in range(2):
        landed(0, half)
        come(12 + half, from_mate.at[pl.ds(2 * half, 2)])
        for k in (2 * half, 2 * half + 1):
            finish(k, total(0, k) + from_mate[k].astype(F32))
    for copy in started:
        copy.wait_send()


def drain(steps, times=None):
    if times is None:
        for _ in steps:
            pass
        return
    for _ in range(times):
        next(steps, None)


def fused_kernel(
    n_row, n_col, scale,
    rows_ref, cols_ref, count_ref, features, weight, cotangent, values,
    out_ref, gw_ref, gf_ref,
    meta_v, meta, vbuf, panel, cslab, slab, stage, acc, aggbuf, gfbuf, sib_in,
    relay_l, relay_r, from_l, from_r, from_mate,
    crelay_l, crelay_r, cfrom_l, cfrom_r, cfrom_mate,
    agg, wterm, wsum, w1, w2, whalf,
    local_sem, agc_s, agc_r, agr_s, agr_r, sib_s, sib_r, rsc_s, rsc_r, rsr_s, rsr_r, sx_s, sx_r,
    ws1_s, ws1_r, ws2_s, ws2_r, ws3_s, ws3_r, wc_s, wc_r,
):
    row = lax.axis_index("row")
    col = lax.axis_index("col")
    core, yl, x = row % 2, (row // 2) % 2, row // 4
    z, yh = col % 4, col // 4
    sibling = {"row": x * 4 + yl * 2 + (1 - core), "col": col}

    load_values = pltpu.make_async_copy(values, vbuf.at[pl.ds(0, NNZ)], local_sem.at[0])
    load_values.start()
    load_own = pltpu.make_async_copy(features, panel.at[pl.ds(col * CHUNK, CHUNK)], local_sem.at[1])
    load_own.start()
    load_cot = pltpu.make_async_copy(cotangent, cslab.at[pl.ds(row * CHUNK, CHUNK)], local_sem.at[2])
    load_cot.start()

    barrier = pltpu.get_barrier_semaphore()

    @pl.loop(1, n_row)
    def _(d):
        pl.semaphore_signal(barrier, inc=1, device_id={"row": (row + d) % n_row, "col": col}, device_id_type=MESH)

    @pl.loop(1, n_col)
    def _(d):
        pl.semaphore_signal(barrier, inc=1, device_id={"row": row, "col": (col + d) % n_col}, device_id_type=MESH)

    vbuf[NNZ] = jnp.zeros((B, B), BF)
    load_own.wait()
    load_cot.wait()
    pl.semaphore_wait(barrier, n_row + n_col - 2)

    ring_c = Ring(z, yh, lambda i, j: j * 4 + i, lambda i, j: {"row": row, "col": j * 4 + i})
    ring_r = Ring(
        x, yl, lambda i, j: i * 4 + j * 2 + core, lambda i, j: {"row": i * 4 + j * 2 + core, "col": col}
    )

    sib_started = []
    sib_taken = []

    def backprop(slot, half):
        piece = pl.ds(slot * CHUNK + 2 * half, 2)
        rows = cslab[piece].reshape(2 * B, cslab.shape[-1])
        grad = lax.dot_general(rows, weight[...], (((1,), (1,)), ((), ())), preferred_element_type=F32)
        slab[piece] = grad.astype(BF).reshape(2, B, cslab.shape[-1])

    def from_sibling(upto):
        while len(sib_taken) < upto:
            index = len(sib_taken)
            slot, half, copy = sib_started[index]
            theirs = slot + 1 - 2 * core
            ref = cslab.at[pl.ds(theirs * CHUNK + 2 * half, 2)]
            remote(ref, ref, sib_s, sib_r, index, sibling).wait_recv()
            backprop(theirs, half)
            sib_taken.append(copy)

    def to_sibling(slot, half):
        index = len(sib_started)
        ref = cslab.at[pl.ds(slot * CHUNK + 2 * half, 2)]
        copy = remote(ref, ref, sib_s, sib_r, index, sibling)
        copy.start()
        backprop(slot, half)
        from_sibling(index - 2)
        sib_started.append((slot, half, copy))

    ag_c = gather_steps(panel, ring_c, agc_s, agc_r, lambda slot, half: None, True)
    ag_r = gather_steps(cslab, ring_r, agr_s, agr_r, to_sibling, False)
    done = object()
    next(ag_c)
    next(ag_r)
    sort_blocks(rows_ref, cols_ref, count_ref, meta_v)
    load_meta = pltpu.make_async_copy(meta_v, meta, local_sem.at[3])
    load_meta.start()
    for index in range(9):
        next(ag_c, done)
        if index >= 1:
            next(ag_r, done)
    drain(ag_c)
    load_values.wait()
    load_meta.wait()
    acc[...] = jnp.zeros_like(acc)
    def forward(t, _):
        a, b = meta[0, BLK + 2 * t], meta[0, BLK + 2 * t + 1]
        ca, cb = meta[0, SRC + 2 * t], meta[0, SRC + 2 * t + 1]
        keep = meta[0, KEEP + t].astype(F32)
        left = jnp.concatenate([vbuf[a], vbuf[b]], axis=1)
        rhs = jnp.concatenate([panel[ca], panel[cb]], axis=0)
        total = acc[...] * keep + jnp.dot(left, rhs, preferred_element_type=F32)
        acc[...] = total
        stage[t] = total.astype(BF)
        return 0

    def backward(t, _):
        a, b = meta[0, META + BLK + 2 * t], meta[0, META + BLK + 2 * t + 1]
        ra, rb = meta[0, META + SRC + 2 * t], meta[0, META + SRC + 2 * t + 1]
        keep = meta[0, META + KEEP + t].astype(F32)
        left = jnp.concatenate([vbuf[a], vbuf[b]], axis=0)
        rhs = jnp.concatenate([slab[ra], slab[rb]], axis=0)
        total = acc[...] * keep + lax.dot_general(
            left, rhs, (((0,), (0,)), ((), ())), preferred_element_type=F32
        )
        acc[...] = total
        stage[t] = total.astype(BF)
        return 0

    f_cut = F_PAIRS // 7
    for piece in range(7):
        lax.fori_loop(piece * f_cut, (piece + 1) * f_cut, forward, 0, unroll=UNROLL)
        next(ag_r, done)
    drain(ag_r)

    def pick(target, slot, base):
        for b in range(CHUNK):
            r = slot * CHUNK + b
            target[r] = stage[meta[0, base + END + r]] * meta[0, base + HAS + r].astype(F32).astype(BF)

    order = [(2, 1), (1, 1), (-1, 1), (2, 0), (1, 0), (-1, 0), (0, 1), (0, 0)]
    swaps = []
    for m, (di, dj) in enumerate(order):
        slot = ring_r.at(di, dj) + 1 - 2 * core
        pick(aggbuf, slot, 0)
        copy = remote(aggbuf.at[pl.ds(slot * CHUNK, CHUNK)], sib_in.at[pl.ds(m * CHUNK, CHUNK)], sx_s, sx_r, m, sibling)
        copy.start()
        swaps.append(copy)
    for di, dj in order:
        pick(aggbuf, ring_r.at(di, dj), 0)

    def ready_r(di, dj):
        m = order.index((di, dj))
        slot = ring_r.at(di, dj)
        ref = sib_in.at[pl.ds(m * CHUNK, CHUNK)]
        remote(ref, ref, sx_s, sx_r, m, sibling).wait_recv()
        for b in range(CHUNK):
            r = slot * CHUNK + b
            aggbuf[r] = (aggbuf[r].astype(F32) + sib_in[m * CHUNK + b].astype(F32)).astype(BF)

    seen = []

    def after_r(di, dj):
        piece = pl.ds(ring_r.at(di, dj) * CHUNK, CHUNK)
        width = aggbuf.shape[-1]
        term = lax.dot_general(
            aggbuf[piece].reshape(CHUNK * B, width), cslab[piece].reshape(CHUNK * B, width),
            (((0,), (0,)), ((), ())), preferred_element_type=F32,
        ).reshape(wterm.shape)
        wterm[...] = wterm[...] + term if seen else term
        seen.append((di, dj))

    def finish_r(k, total):
        agg[k] = total.astype(BF)

    def finish_c(k, total):
        gf_ref[k] = total.astype(BF)

    rs_r = scatter_steps(
        aggbuf, ring_r, rsr_s, rsr_r, relay_l, relay_r, from_l, from_r, from_mate, ready_r, after_r, finish_r
    )
    acc[...] = jnp.zeros_like(acc)
    from_sibling(16)
    for copy in sib_taken:
        copy.wait_send()
    for piece in range(13):
        lax.fori_loop(piece * UNROLL, (piece + 1) * UNROLL, backward, 0, unroll=UNROLL)
        if piece in (0, 1, 2):
            drain(rs_r, 1)
    rs_c = scatter_steps(
        gfbuf, ring_c, rsc_s, rsc_r, crelay_l, crelay_r, cfrom_l, cfrom_r, cfrom_mate,
        lambda di, dj: pick(gfbuf, ring_c.at(di, dj), META), lambda di, dj: None, finish_c,
    )
    spot = x * 2 + yl
    n_chip = n_row // 2

    def chip(d):
        other = (spot + d) % n_chip
        return other, {"row": other * 2 + core, "col": col}

    def w1_copy(d):
        other, device = chip(d)
        return remote(wterm.at[core, other], w1.at[d - 1], ws1_s, ws1_r, d - 1, device)

    def w2_copy(d):
        target = (col + d) % n_col
        return remote(w2.at[col], w2.at[col], ws2_s, ws2_r, d - 1, {"row": row, "col": target})

    def w3_copy(d):
        _, device = chip(d)
        return remote(wsum.at[core, spot], wsum.at[core, spot], ws3_s, ws3_r, d - 1, device)

    drain(rs_r, 2)
    drain(rs_c, 3)
    drain(rs_r, 4)
    to_core = remote(wterm.at[1 - core], whalf, wc_s, wc_r, 0, sibling)
    to_core.start()
    drain(rs_c, 2)
    to_core.wait_recv()
    wterm[core] = wterm[core] + whalf[...]
    for d in range(1, n_chip):
        w1_copy(d).start()
    drain(rs_r, 1)
    drain(rs_c, 3)
    drain(rs_r, 2)
    share = wterm[core, spot]
    for d in range(1, n_chip):
        w1_copy(d).wait_recv()
        share = share + w1[d - 1]
    w2[col] = share
    for d in range(1, n_col):
        w2_copy(d).start()
    drain(rs_c, 1)
    for d in range(1, n_col):
        origin = (col + n_col - d) % n_col
        remote(w2.at[origin], w2.at[origin], ws2_s, ws2_r, d - 1, sibling).wait_recv()
    whole = w2[0]
    for c in range(1, n_col):
        whole = whole + w2[c]
    wsum[core, spot] = whole * scale
    for d in range(1, n_chip):
        w3_copy(d).start()
    drain(rs_c, 1)
    drain(rs_c, 2)
    drain(rs_r)
    for copy in swaps:
        copy.wait_send()
    for b in range(CHUNK):
        out_ref[b] = jnp.dot(agg[b], weight[...], preferred_element_type=F32).astype(BF)
    for d in range(1, n_chip):
        origin = (spot + n_chip - d) % n_chip
        remote(wsum.at[core, origin], wsum.at[core, origin], ws3_s, ws3_r, d - 1, sibling).wait_recv()
    back = remote(wsum.at[core], wsum.at[core], wc_s, wc_r, 1, sibling)
    back.start()
    drain(rs_c)
    remote(wsum.at[1 - core], wsum.at[1 - core], wc_s, wc_r, 1, sibling).wait_recv()
    gw_ref[...] = wsum[...]
    for d in range(1, n_chip):
        w1_copy(d).wait_send()
        w3_copy(d).wait_send()
    for d in range(1, n_col):
        w2_copy(d).wait_send()
    to_core.wait_send()
    back.wait_send()


def body(features, weight, cotangent, block_rows, block_cols, counts, values):
    n_row = lax.axis_size("row")
    n_col = lax.axis_size("col")
    width = features.shape[-1]
    nodes = features.shape[0] * n_row * n_col
    shard = (CHUNK, B, width)

    def vm(*shape, dtype=BF):
        return pltpu.VMEM(shape, dtype)

    dma = pltpu.SemaphoreType.DMA
    wide = (B, width)
    scratch = [
        vm(1, 2 * META, dtype=jnp.int32), pltpu.SMEM((1, 2 * META), jnp.int32),
        vm(NNZ + 1, B, B), vm(CHUNK * n_col, *wide), vm(CHUNK * n_row, *wide), vm(CHUNK * n_row, *wide), vm(F_PAIRS, *wide),
        vm(*wide, dtype=F32), vm(CHUNK * n_row, *wide), vm(CHUNK * n_col, *wide), vm(CHUNK * n_row // 2, *wide),
        vm(2, 2, *wide), vm(2, 2, *wide), vm(2, CHUNK, *wide), vm(2, CHUNK, *wide), vm(*shard),
        vm(2, 2, *wide), vm(2, 2, *wide), vm(2, CHUNK, *wide), vm(2, CHUNK, *wide), vm(*shard),
        vm(*shard),
        vm(2, n_row // 2, width // n_row, width, dtype=F32), vm(2, n_row // 2, width // n_row, width, dtype=F32),
        vm(n_row // 2 - 1, width // n_row, width, dtype=F32), vm(n_col, width // n_row, width, dtype=F32),
        vm(n_row // 2, width // n_row, width, dtype=F32),
        dma((4,)), dma((14,)), dma((14,)), dma((14,)), dma((14,)), dma((16,)), dma((16,)),
        dma((14,)), dma((14,)), dma((14,)), dma((14,)), dma((8,)), dma((8,)),
        dma((n_row // 2 - 1,)), dma((n_row // 2 - 1,)), dma((n_col - 1,)), dma((n_col - 1,)),
        dma((n_row // 2 - 1,)), dma((n_row // 2 - 1,)), dma((2,)), dma((2,)),
    ]
    vmem = pl.BlockSpec(memory_space=pltpu.VMEM)
    out, gw, gf = pl.pallas_call(
        functools.partial(fused_kernel, n_row, n_col, float(nodes) ** -0.5),
        out_shape=[
            jax.ShapeDtypeStruct(shard, BF),
            jax.ShapeDtypeStruct((2, n_row // 2, width // n_row, width), F32),
            jax.ShapeDtypeStruct(shard, BF),
        ],
        in_specs=[vmem, vmem, pl.BlockSpec(memory_space=pltpu.SMEM), pl.BlockSpec(memory_space=pl.ANY), vmem] + [pl.BlockSpec(memory_space=pl.ANY)] * 2,
        out_specs=[vmem] * 3,
        scratch_shapes=scratch,
        compiler_params=pltpu.CompilerParams(
            collective_id=0, has_side_effects=True, vmem_limit_bytes=60 * 1024 * 1024
        ),
    )(block_rows[0], block_cols[0], counts, features.reshape(shard), weight, cotangent.reshape(shard), values[0, 0])
    out, gw, gf = pl.pallas_call(
        hand_over,
        out_shape=[jax.ShapeDtypeStruct(item.shape, item.dtype) for item in (out, gw, gf)],
        in_specs=[vmem] * 3,
        out_specs=[vmem] * 3,
    )(out, gw, gf)
    return out.reshape(features.shape), gw.reshape(width, width), gf.reshape(features.shape)


def solution(mesh):
    placed = (
        P(("row", "col"), None),
        P(),
        P(("col", "row"), None),
        P("row", "col", None),
        P("row", "col", None),
        P("row", "col"),
        P("row", "col", None, None, None),
    )
    return jax.shard_map(
        body,
        mesh=mesh,
        in_specs=placed,
        out_specs=(P(("col", "row"), None), P(), P(("row", "col"), None)),
        check_vma=False,
    )
```

```python
import functools

import jax
import jax.numpy as jnp
from jax import lax
from jax.experimental import pallas as pl
from jax.experimental.pallas import tpu as pltpu
from jax.sharding import PartitionSpec as P

MESH = pl.DeviceIdType.MESH
BF = jnp.bfloat16
F32 = jnp.float32
B = 128
NNZ = 384
SLOTS = 512
F_PAIRS = 224
B_PAIRS = 208
CHUNK = 4
UNROLL = 16
BLK, SRC, KEEP, END, HAS, META = 0, 512, 1024, 1280, 1408, 1536


def sort_blocks(rows_ref, cols_ref, count_ref, meta):
    count = count_ref[0, 0]

    def iota(shape, axis):
        return lax.broadcasted_iota(jnp.int32, shape, axis)

    valid = iota((1, NNZ), 1) < count
    rows = jnp.where(valid, rows_ref[...], 900)
    cols = jnp.where(valid, cols_ref[...], 900)
    rows_t = jnp.transpose(jnp.broadcast_to(rows, (B, NNZ)))
    cols_t = jnp.transpose(jnp.broadcast_to(cols, (B, NNZ)))
    sub_k = iota((NNZ, B), 0)
    lane_r = iota((NNZ, B), 1)
    earlier = iota((NNZ, NNZ), 0) < iota((NNZ, NNZ), 1)
    sub_r = iota((B, NNZ), 0)
    sub_q = iota((B, B), 0)
    lane_q = iota((B, B), 1)

    def count_up(mask, axis):
        return jnp.sum(jnp.where(mask, 1, 0), axis=axis, keepdims=True)

    def one(key, key_t, src_t, base):
        key_tt = jnp.concatenate([key_t] * (NNZ // B), axis=1)
        within = count_up((key_tt == jnp.broadcast_to(key, (NNZ, NNZ))) & earlier, 0)
        n_l = count_up(key_t == lane_r, 0)
        hot = sub_r == jnp.broadcast_to(key, (B, NNZ))
        n_s = count_up(hot, 1)
        q_l = (n_l + 1) >> 1
        q_s = (n_s + 1) >> 1
        s_l = jnp.sum(jnp.where(sub_q < lane_q, jnp.broadcast_to(q_s, (B, B)), 0), axis=0, keepdims=True)
        s_s = jnp.sum(jnp.where(lane_q < sub_q, jnp.broadcast_to(q_l, (B, B)), 0), axis=1, keepdims=True)
        slot = 2 * jnp.sum(jnp.where(hot, jnp.broadcast_to(s_s, (B, NNZ)), 0), axis=0, keepdims=True) + within
        slot = jnp.where(valid, slot, 9000)
        slot_t = jnp.transpose(jnp.broadcast_to(slot, (B, NNZ)))
        src_clean = jnp.where(src_t < 800, src_t, 0)
        for part in range(SLOTS // B):
            match = slot_t == lane_r + part * B
            found = jnp.sum(jnp.where(match, sub_k + 1, 0), axis=0, keepdims=True)
            where = jnp.sum(jnp.where(match, src_clean, 0), axis=0, keepdims=True)
            meta[:, pl.ds(base + BLK + part * B, B)] = jnp.where(found == 0, NNZ, found - 1)
            meta[:, pl.ds(base + SRC + part * B, B)] = where
        for part in range(2):
            first = (s_s == lane_q + part * B) & (n_s > 0)
            meta[:, pl.ds(base + KEEP + part * B, B)] = 1 - count_up(first, 0)
        meta[:, pl.ds(base + END, B)] = jnp.where(n_l > 0, s_l + q_l - 1, 0)
        meta[:, pl.ds(base + HAS, B)] = jnp.where(n_l > 0, 1, 0)

    one(rows, rows_t, cols_t, 0)
    one(cols, cols_t, rows_t, META)


def hand_over(src_a, src_b, src_c, dst_a, dst_b, dst_c):
    dst_a[...] = src_a[...]
    dst_b[...] = src_b[...]
    dst_c[...] = src_c[...]


class Ring:
    def __init__(self, i, j, slot, device):
        self.i, self.j, self.slot, self.device = i, j, slot, device

    def at(self, di, dj):
        i = (self.i + di + 4) % 4
        j = self.j if dj == 0 else 1 - self.j
        return self.slot(i, j)

    def dev(self, di, dj):
        i = (self.i + di + 4) % 4
        j = self.j if dj == 0 else 1 - self.j
        return self.device(i, j)


def remote(src, dst, send, recv, index, device):
    return pltpu.make_async_remote_copy(
        src_ref=src, dst_ref=dst, send_sem=send.at[index], recv_sem=recv.at[index], device_id=device, device_id_type=MESH
    )


def gather_steps(buf, ring, send, recv, arrived, pair_first):
    def part(slot, half):
        return buf.at[pl.ds(slot * CHUNK + 2 * half, 2)]

    right, left, mate = ring.dev(1, 0), ring.dev(-1, 0), ring.dev(0, 1)
    started = []

    def go(index, slot, half, device):
        copy = remote(part(slot, half), part(slot, half), send, recv, index, device)
        copy.start()
        started.append(copy)

    def come(index, slot, half):
        remote(part(slot, half), part(slot, half), send, recv, index, right).wait_recv()
        arrived(slot, half)

    own, other = ring.at(0, 0), ring.at(0, 1)
    if pair_first:
        go(0, own, 0, mate)
    go(2, own, 0, right)
    go(8, own, 1, left)
    if pair_first:
        go(1, own, 1, mate)
    go(3, own, 1, right)
    go(9, own, 0, left)
    arrived(own, 0)
    arrived(own, 1)
    yield
    come(2, ring.at(-1, 0), 0)
    go(6, ring.at(-1, 0), 0, right)
    if not pair_first:
        go(0, own, 0, mate)
        go(1, own, 1, mate)
    yield
    come(8, ring.at(1, 0), 1)
    go(12, ring.at(1, 0), 1, left)
    yield
    come(0, other, 0)
    go(4, other, 0, right)
    go(11, other, 0, left)
    yield
    come(1, other, 1)
    go(10, other, 1, left)
    go(5, other, 1, right)
    yield
    come(3, ring.at(-1, 0), 1)
    come(9, ring.at(1, 0), 0)
    yield
    come(4, ring.at(-1, 1), 0)
    go(7, ring.at(-1, 1), 0, right)
    yield
    come(10, ring.at(1, 1), 1)
    go(13, ring.at(1, 1), 1, left)
    yield
    come(6, ring.at(-2, 0), 0)
    come(12, ring.at(2, 0), 1)
    yield
    come(5, ring.at(-1, 1), 1)
    come(11, ring.at(1, 1), 0)
    yield
    come(7, ring.at(-2, 1), 0)
    come(13, ring.at(2, 1), 1)
    for copy in started:
        copy.wait_send()


def scatter_steps(buf, ring, send, recv, relay_l, relay_r, from_l, from_r, from_mate, ready, after, finish):
    right, left, mate = ring.dev(1, 0), ring.dev(-1, 0), ring.dev(0, 1)
    started = []

    def part(slot, half):
        return buf.at[pl.ds(slot * CHUNK + 2 * half, 2)]

    def go(index, src, dst, device):
        copy = remote(src, dst, send, recv, index, device)
        copy.start()
        started.append(copy)

    def come(index, ref):
        remote(ref, ref, send, recv, index, right).wait_recv()

    def add(slot, half, ref):
        view = part(slot, half)
        for b in range(2):
            view[b] = (view[b].astype(F32) + ref[b].astype(F32)).astype(BF)

    def feed(dj):
        ready(2, dj)
        slot = ring.at(2, dj)
        go(0 + dj, part(slot, 0), relay_l.at[dj], right)
        go(2 + dj, part(slot, 1), relay_r.at[dj], left)
        after(2, dj)
        yield
        ready(1, dj)
        go(4 + dj, part(ring.at(1, dj), 1), from_l.at[dj, pl.ds(2, 2)], right)
        after(1, dj)
        yield
        ready(-1, dj)
        go(6 + dj, part(ring.at(-1, dj), 0), from_r.at[dj, pl.ds(0, 2)], left)
        after(-1, dj)
        yield

    def relay(dj):
        come(0 + dj, relay_l.at[dj])
        add(ring.at(1, dj), 0, relay_l.at[dj])
        go(8 + dj, part(ring.at(1, dj), 0), from_l.at[dj, pl.ds(0, 2)], right)
        yield
        come(2 + dj, relay_r.at[dj])
        add(ring.at(-1, dj), 1, relay_r.at[dj])
        go(10 + dj, part(ring.at(-1, dj), 1), from_r.at[dj, pl.ds(2, 2)], left)
        yield

    def landed(dj, half):
        piece = pl.ds(2 * half, 2)
        come((8 if half == 0 else 4) + dj, from_l.at[dj, piece])
        come((6 if half == 0 else 10) + dj, from_r.at[dj, piece])

    def total(dj, k):
        r = ring.at(0, dj) * CHUNK + k
        return buf[r].astype(F32) + from_l[dj, k].astype(F32) + from_r[dj, k].astype(F32)

    yield from feed(1)
    yield from relay(1)
    yield from feed(0)
    for dj in (1, 0):
        ready(0, dj)
        after(0, dj)
    yield
    for half in range(2):
        landed(1, half)
        for k in (2 * half, 2 * half + 1):
            buf[ring.at(0, 1) * CHUNK + k] = total(1, k).astype(BF)
        go(12 + half, part(ring.at(0, 1), half), from_mate.at[pl.ds(2 * half, 2)], mate)
    yield
    yield from relay(0)
    for half in range(2):
        landed(0, half)
        come(12 + half, from_mate.at[pl.ds(2 * half, 2)])
        for k in (2 * half, 2 * half + 1):
            finish(k, total(0, k) + from_mate[k].astype(F32))
    for copy in started:
        copy.wait_send()


def drain(steps, times=None):
    if times is None:
        for _ in steps:
            pass
        return
    for _ in range(times):
        next(steps, None)


def fused_kernel(
    n_row, n_col, scale,
    rows_ref, cols_ref, count_ref, features, weight, cotangent, values,
    out_ref, gw_ref, gf_ref,
    meta_v, meta, vbuf, panel, cslab, slab, stage, acc, aggbuf, gfbuf, sib_in,
    relay_l, relay_r, from_l, from_r, from_mate,
    crelay_l, crelay_r, cfrom_l, cfrom_r, cfrom_mate,
    agg, wterm, wsum, w1, w2, whalf,
    local_sem, agc_s, agc_r, agr_s, agr_r, sib_s, sib_r, rsc_s, rsc_r, rsr_s, rsr_r, sx_s, sx_r,
    ws1_s, ws1_r, ws2_s, ws2_r, ws3_s, ws3_r, wc_s, wc_r,
):
    row = lax.axis_index("row")
    col = lax.axis_index("col")
    core, yl, x = row % 2, (row // 2) % 2, row // 4
    z, yh = col % 4, col // 4
    sibling = {"row": x * 4 + yl * 2 + (1 - core), "col": col}

    load_values = pltpu.make_async_copy(values, vbuf.at[pl.ds(0, NNZ)], local_sem.at[0])
    load_values.start()
    load_own = pltpu.make_async_copy(features, panel.at[pl.ds(col * CHUNK, CHUNK)], local_sem.at[1])
    load_own.start()
    load_cot = pltpu.make_async_copy(cotangent, cslab.at[pl.ds(row * CHUNK, CHUNK)], local_sem.at[2])
    load_cot.start()

    barrier = pltpu.get_barrier_semaphore()

    @pl.loop(1, n_row)
    def _(d):
        pl.semaphore_signal(barrier, inc=1, device_id={"row": (row + d) % n_row, "col": col}, device_id_type=MESH)

    @pl.loop(1, n_col)
    def _(d):
        pl.semaphore_signal(barrier, inc=1, device_id={"row": row, "col": (col + d) % n_col}, device_id_type=MESH)

    vbuf[NNZ] = jnp.zeros((B, B), BF)
    load_own.wait()
    load_cot.wait()
    pl.semaphore_wait(barrier, n_row + n_col - 2)

    ring_c = Ring(z, yh, lambda i, j: j * 4 + i, lambda i, j: {"row": row, "col": j * 4 + i})
    ring_r = Ring(
        x, yl, lambda i, j: i * 4 + j * 2 + core, lambda i, j: {"row": i * 4 + j * 2 + core, "col": col}
    )

    sib_started = []
    sib_taken = []

    def backprop(slot, half):
        piece = pl.ds(slot * CHUNK + 2 * half, 2)
        rows = cslab[piece].reshape(2 * B, cslab.shape[-1])
        grad = lax.dot_general(rows, weight[...], (((1,), (1,)), ((), ())), preferred_element_type=F32)
        slab[piece] = grad.astype(BF).reshape(2, B, cslab.shape[-1])

    def from_sibling(upto):
        while len(sib_taken) < upto:
            index = len(sib_taken)
            slot, half, copy = sib_started[index]
            theirs = slot + 1 - 2 * core
            ref = cslab.at[pl.ds(theirs * CHUNK + 2 * half, 2)]
            remote(ref, ref, sib_s, sib_r, index, sibling).wait_recv()
            backprop(theirs, half)
            sib_taken.append(copy)

    def to_sibling(slot, half):
        index = len(sib_started)
        ref = cslab.at[pl.ds(slot * CHUNK + 2 * half, 2)]
        copy = remote(ref, ref, sib_s, sib_r, index, sibling)
        copy.start()
        backprop(slot, half)
        from_sibling(index - 2)
        sib_started.append((slot, half, copy))

    ag_c = gather_steps(panel, ring_c, agc_s, agc_r, lambda slot, half: None, True)
    ag_r = gather_steps(cslab, ring_r, agr_s, agr_r, to_sibling, False)
    done = object()
    next(ag_c)
    next(ag_r)
    sort_blocks(rows_ref, cols_ref, count_ref, meta_v)
    load_meta = pltpu.make_async_copy(meta_v, meta, local_sem.at[3])
    load_meta.start()
    for index in range(9):
        next(ag_c, done)
        if index >= 1:
            next(ag_r, done)
    drain(ag_c)
    load_values.wait()
    load_meta.wait()
    acc[...] = jnp.zeros_like(acc)
    def forward(t, _):
        a, b = meta[0, BLK + 2 * t], meta[0, BLK + 2 * t + 1]
        ca, cb = meta[0, SRC + 2 * t], meta[0, SRC + 2 * t + 1]
        keep = meta[0, KEEP + t].astype(F32)
        left = jnp.concatenate([vbuf[a], vbuf[b]], axis=1)
        rhs = jnp.concatenate([panel[ca], panel[cb]], axis=0)
        total = acc[...] * keep + jnp.dot(left, rhs, preferred_element_type=F32)
        acc[...] = total
        stage[t] = total.astype(BF)
        return 0

    def backward(t, _):
        a, b = meta[0, META + BLK + 2 * t], meta[0, META + BLK + 2 * t + 1]
        ra, rb = meta[0, META + SRC + 2 * t], meta[0, META + SRC + 2 * t + 1]
        keep = meta[0, META + KEEP + t].astype(F32)
        left = jnp.concatenate([vbuf[a], vbuf[b]], axis=0)
        rhs = jnp.concatenate([slab[ra], slab[rb]], axis=0)
        total = acc[...] * keep + lax.dot_general(
            left, rhs, (((0,), (0,)), ((), ())), preferred_element_type=F32
        )
        acc[...] = total
        stage[t] = total.astype(BF)
        return 0

    f_cut = F_PAIRS // 7
    for piece in range(7):
        lax.fori_loop(piece * f_cut, (piece + 1) * f_cut, forward, 0, unroll=UNROLL)
        next(ag_r, done)
    drain(ag_r)

    def pick(target, slot, base):
        for b in range(CHUNK):
            r = slot * CHUNK + b
            target[r] = stage[meta[0, base + END + r]] * meta[0, base + HAS + r].astype(F32).astype(BF)

    order = [(2, 1), (1, 1), (-1, 1), (2, 0), (1, 0), (-1, 0), (0, 1), (0, 0)]
    swaps = []
    for group in (order[:3], order[3:]):
        for di, dj in group:
            m = order.index((di, dj))
            slot = ring_r.at(di, dj) + 1 - 2 * core
            pick(aggbuf, slot, 0)
            copy = remote(
                aggbuf.at[pl.ds(slot * CHUNK, CHUNK)], sib_in.at[pl.ds(m * CHUNK, CHUNK)], sx_s, sx_r, m, sibling
            )
            copy.start()
            swaps.append(copy)
        for di, dj in group:
            pick(aggbuf, ring_r.at(di, dj), 0)

    def ready_r(di, dj):
        m = order.index((di, dj))
        slot = ring_r.at(di, dj)
        ref = sib_in.at[pl.ds(m * CHUNK, CHUNK)]
        remote(ref, ref, sx_s, sx_r, m, sibling).wait_recv()
        for b in range(CHUNK):
            r = slot * CHUNK + b
            aggbuf[r] = (aggbuf[r].astype(F32) + sib_in[m * CHUNK + b].astype(F32)).astype(BF)

    seen = []

    def after_r(di, dj):
        piece = pl.ds(ring_r.at(di, dj) * CHUNK, CHUNK)
        width = aggbuf.shape[-1]
        term = lax.dot_general(
            aggbuf[piece].reshape(CHUNK * B, width), cslab[piece].reshape(CHUNK * B, width),
            (((0,), (0,)), ((), ())), preferred_element_type=F32,
        ).reshape(wterm.shape)
        wterm[...] = wterm[...] + term if seen else term
        seen.append((di, dj))

    def finish_r(k, total):
        agg[k] = total.astype(BF)

    def finish_c(k, total):
        gf_ref[k] = total.astype(BF)

    rs_r = scatter_steps(
        aggbuf, ring_r, rsr_s, rsr_r, relay_l, relay_r, from_l, from_r, from_mate, ready_r, after_r, finish_r
    )
    acc[...] = jnp.zeros_like(acc)
    from_sibling(16)
    for copy in sib_taken:
        copy.wait_send()
    for piece in range(13):
        if piece in (0, 1, 2):
            drain(rs_r, 1)
        lax.fori_loop(piece * UNROLL, (piece + 1) * UNROLL, backward, 0, unroll=UNROLL)
    rs_c = scatter_steps(
        gfbuf, ring_c, rsc_s, rsc_r, crelay_l, crelay_r, cfrom_l, cfrom_r, cfrom_mate,
        lambda di, dj: pick(gfbuf, ring_c.at(di, dj), META), lambda di, dj: None, finish_c,
    )
    spot = x * 2 + yl
    n_chip = n_row // 2

    def chip(d):
        other = (spot + d) % n_chip
        return other, {"row": other * 2 + core, "col": col}

    def w1_copy(d):
        other, device = chip(d)
        return remote(wterm.at[core, other], w1.at[d - 1], ws1_s, ws1_r, d - 1, device)

    def w2_copy(d):
        target = (col + d) % n_col
        return remote(w2.at[col], w2.at[col], ws2_s, ws2_r, d - 1, {"row": row, "col": target})

    def w3_copy(d):
        _, device = chip(d)
        return remote(wsum.at[core, spot], wsum.at[core, spot], ws3_s, ws3_r, d - 1, device)

    drain(rs_c, 3)
    drain(rs_r, 6)
    to_core = remote(wterm.at[1 - core], whalf, wc_s, wc_r, 0, sibling)
    to_core.start()
    drain(rs_c, 2)
    to_core.wait_recv()
    wterm[core] = wterm[core] + whalf[...]
    for d in range(1, n_chip):
        w1_copy(d).start()
    drain(rs_r, 1)
    drain(rs_c, 3)
    drain(rs_r, 2)
    share = wterm[core, spot]
    for d in range(1, n_chip):
        w1_copy(d).wait_recv()
        share = share + w1[d - 1]
    w2[col] = share
    for d in range(1, n_col):
        w2_copy(d).start()
    drain(rs_c, 1)
    for d in range(1, n_col):
        origin = (col + n_col - d) % n_col
        remote(w2.at[origin], w2.at[origin], ws2_s, ws2_r, d - 1, sibling).wait_recv()
    whole = w2[0]
    for c in range(1, n_col):
        whole = whole + w2[c]
    wsum[core, spot] = whole * scale
    for d in range(1, n_chip):
        w3_copy(d).start()
    drain(rs_c, 1)
    drain(rs_c, 2)
    drain(rs_r)
    for copy in swaps:
        copy.wait_send()
    for b in range(CHUNK):
        out_ref[b] = jnp.dot(agg[b], weight[...], preferred_element_type=F32).astype(BF)
    for d in range(1, n_chip):
        origin = (spot + n_chip - d) % n_chip
        remote(wsum.at[core, origin], wsum.at[core, origin], ws3_s, ws3_r, d - 1, sibling).wait_recv()
    back = remote(wsum.at[core], wsum.at[core], wc_s, wc_r, 1, sibling)
    back.start()
    drain(rs_c)
    remote(wsum.at[1 - core], wsum.at[1 - core], wc_s, wc_r, 1, sibling).wait_recv()
    gw_ref[...] = wsum[...]
    for d in range(1, n_chip):
        w1_copy(d).wait_send()
        w3_copy(d).wait_send()
    for d in range(1, n_col):
        w2_copy(d).wait_send()
    to_core.wait_send()
    back.wait_send()


def body(features, weight, cotangent, block_rows, block_cols, counts, values):
    n_row = lax.axis_size("row")
    n_col = lax.axis_size("col")
    width = features.shape[-1]
    nodes = features.shape[0] * n_row * n_col
    shard = (CHUNK, B, width)

    def vm(*shape, dtype=BF):
        return pltpu.VMEM(shape, dtype)

    dma = pltpu.SemaphoreType.DMA
    wide = (B, width)
    scratch = [
        vm(1, 2 * META, dtype=jnp.int32), pltpu.SMEM((1, 2 * META), jnp.int32),
        vm(NNZ + 1, B, B), vm(CHUNK * n_col, *wide), vm(CHUNK * n_row, *wide), vm(CHUNK * n_row, *wide), vm(F_PAIRS, *wide),
        vm(*wide, dtype=F32), vm(CHUNK * n_row, *wide), vm(CHUNK * n_col, *wide), vm(CHUNK * n_row // 2, *wide),
        vm(2, 2, *wide), vm(2, 2, *wide), vm(2, CHUNK, *wide), vm(2, CHUNK, *wide), vm(*shard),
        vm(2, 2, *wide), vm(2, 2, *wide), vm(2, CHUNK, *wide), vm(2, CHUNK, *wide), vm(*shard),
        vm(*shard),
        vm(2, n_row // 2, width // n_row, width, dtype=F32), vm(2, n_row // 2, width // n_row, width, dtype=F32),
        vm(n_row // 2 - 1, width // n_row, width, dtype=F32), vm(n_col, width // n_row, width, dtype=F32),
        vm(n_row // 2, width // n_row, width, dtype=F32),
        dma((4,)), dma((14,)), dma((14,)), dma((14,)), dma((14,)), dma((16,)), dma((16,)),
        dma((14,)), dma((14,)), dma((14,)), dma((14,)), dma((8,)), dma((8,)),
        dma((n_row // 2 - 1,)), dma((n_row // 2 - 1,)), dma((n_col - 1,)), dma((n_col - 1,)),
        dma((n_row // 2 - 1,)), dma((n_row // 2 - 1,)), dma((2,)), dma((2,)),
    ]
    vmem = pl.BlockSpec(memory_space=pltpu.VMEM)
    out, gw, gf = pl.pallas_call(
        functools.partial(fused_kernel, n_row, n_col, float(nodes) ** -0.5),
        out_shape=[
            jax.ShapeDtypeStruct(shard, BF),
            jax.ShapeDtypeStruct((2, n_row // 2, width // n_row, width), F32),
            jax.ShapeDtypeStruct(shard, BF),
        ],
        in_specs=[vmem, vmem, pl.BlockSpec(memory_space=pltpu.SMEM), pl.BlockSpec(memory_space=pl.ANY), vmem] + [pl.BlockSpec(memory_space=pl.ANY)] * 2,
        out_specs=[vmem] * 3,
        scratch_shapes=scratch,
        compiler_params=pltpu.CompilerParams(
            collective_id=0, has_side_effects=True, vmem_limit_bytes=60 * 1024 * 1024
        ),
    )(block_rows[0], block_cols[0], counts, features.reshape(shard), weight, cotangent.reshape(shard), values[0, 0])
    out, gw, gf = pl.pallas_call(
        hand_over,
        out_shape=[jax.ShapeDtypeStruct(item.shape, item.dtype) for item in (out, gw, gf)],
        in_specs=[vmem] * 3,
        out_specs=[vmem] * 3,
    )(out, gw, gf)
    return out.reshape(features.shape), gw.reshape(width, width), gf.reshape(features.shape)


def solution(mesh):
    placed = (
        P(("row", "col"), None),
        P(),
        P(("col", "row"), None),
        P("row", "col", None),
        P("row", "col", None),
        P("row", "col"),
        P("row", "col", None, None, None),
    )
    return jax.shard_map(
        body,
        mesh=mesh,
        in_specs=placed,
        out_specs=(P(("col", "row"), None), P(), P(("row", "col"), None)),
        check_vma=False,
    )
```
